128 devices in a mesh: fsdp: 8 (over y, z_lo), tensor: 16 (over x, z_hi, core).
Axes of the slice: x: 4, y: 4, z: 4 (z_hi: 2, z_lo: 2; z = z_hi * 2 + z_lo), core: 2. Of those that a mesh axis runs over, the one named last changes fastest.
Arguments:
- tokens: bfloat16 [16384, 1024], P(('fsdp', 'tensor')), may hold values from -6 to 6
- cotangent: bfloat16 [16384, 1024], P(('fsdp', 'tensor')), may hold values from -6 to 6
- w_qkv: bfloat16 [2, 1024, 16, 192], P(None, 'fsdp', 'tensor'), may hold values from -0.1875 to 0.1875
- qv_bias: bfloat16 [2, 16, 128], P(None, 'tensor'), may hold values from -3 to 3
- w_out: bfloat16 [2, 16, 64, 1024], P(None, 'tensor', None, 'fsdp'), may hold values from -0.75 to 0.75
- w_fc1: bfloat16 [2, 1024, 4096], P(None, 'fsdp', 'tensor'), may hold values from -0.1875 to 0.1875
- fc1_bias: bfloat16 [2, 4096], P(None, 'tensor'), may hold values from -3 to 3
- w_fc2: bfloat16 [2, 4096, 1024], P(None, 'tensor', 'fsdp'), may hold values from -0.09375 to 0.09375
- norm_gain: bfloat16 [2, 2, 1024], P(None, None, 'fsdp'), may hold values from 0.25 to 1.75
- norm_bias: bfloat16 [2, 2, 1024], P(None, None, 'fsdp'), may hold values from -2 to 2
- layer_scale: bfloat16 [2, 2, 1024], P(None, None, 'fsdp'), may hold values from 0.5 to 1.5
- out_bias: bfloat16 [2, 2, 1024], P(None, None, 'fsdp'), may hold values from -2 to 2
Outputs:
- out_tokens: bfloat16 [16384, 1024], P(('fsdp', 'tensor'))
- grad_tokens: float32 [16384, 1024], P(('fsdp', 'tensor'))
- grad_w_qkv: float32 [2, 1024, 16, 192], P(None, 'fsdp', 'tensor')
- grad_qv_bias: float32 [2, 16, 128], P(None, 'tensor')
- grad_w_out: float32 [2, 16, 64, 1024], P(None, 'tensor', None, 'fsdp')
- grad_w_fc1: float32 [2, 1024, 4096], P(None, 'fsdp', 'tensor')
- grad_fc1_bias: float32 [2, 4096], P(None, 'tensor')
- grad_w_fc2: float32 [2, 4096, 1024], P(None, 'tensor', 'fsdp')
- grad_norm_gain: float32 [2, 2, 1024], P(None, None, 'fsdp')
- grad_norm_bias: float32 [2, 2, 1024], P(None, None, 'fsdp')
- grad_layer_scale: float32 [2, 2, 1024], P(None, None, 'fsdp')
- grad_out_bias: float32 [2, 2, 1024], P(None, None, 'fsdp')
The draws below stay inside these ranges and needn't reach their ends.
All inputs are finite; a program needn't handle non-finite values.
Results may differ from the reference program's by a relative error of at most 0.02.
Values may be sent and summed in bfloat16 or wider, within the bound.
A program may use at most 192 MiB of HBM per device.

```python
import math
import jax
import jax.numpy as jnp
from jax import lax

D = 1024
H = 16
HD = 64
FF = 4096
L = 2
SEQ = 1024
TOKENS = 16384


def levels(own_key, shape, pieces, low, largest):
    factor_of = 1.0
    for axis_at, parts in pieces:
        heights = jax.random.uniform(jax.random.fold_in(jax.random.fold_in(own_key, 6), axis_at), (parts,), jnp.float32, low / len(pieces), largest / len(pieces))
        factor_of = factor_of * jnp.repeat(jnp.exp(heights), shape[axis_at] // parts).reshape((-1,) + (1,) * (len(shape) - 1 - axis_at))
    return factor_of


def noise(key, extent, deviation, reach, pieces=(), dtype=jnp.bfloat16):
    level = levels(key, extent, pieces, -0.22, 0.18) if pieces else 1.0
    entries = jax.random.normal(key, extent, jnp.float32) * deviation * level
    return jnp.minimum(jnp.maximum(entries, -reach), reach).astype(dtype)


def setup_inputs(seed: int = 0) -> dict:
    arg_keys = jax.random.split(jax.random.key(seed), 13)
    return {
        "tokens": noise(arg_keys[0], (TOKENS, D), 1.0, 6.0, ((0, 128),)),
        "cotangent": noise(arg_keys[1], (TOKENS, D), 1.0, 6.0, ((0, 128),)),
        "w_qkv": noise(arg_keys[2], (L, D, H, 3 * HD), D ** -0.5, 0.1875, ((1, 8), (2, 16))),
        "qv_bias": noise(arg_keys[3], (L, H, 2 * HD), 0.5, 3.0, ((1, 16),)),
        "w_out": noise(arg_keys[4], (L, H, HD, D), HD ** -0.5, 0.75, ((1, 16), (3, 8))),
        "w_fc1": noise(arg_keys[5], (L, D, FF), D ** -0.5, 0.1875, ((1, 8), (2, 16))),
        "fc1_bias": noise(arg_keys[6], (L, FF), 0.5, 3.0, ((1, 16),)),
        "w_fc2": noise(arg_keys[7], (L, FF, D), FF ** -0.5, 0.09375, ((1, 16), (2, 8))),
        "norm_gain": jnp.clip(1.0 + 0.15 * jax.random.normal(arg_keys[8], (L, 2, D), jnp.float32), 0.25, 1.75).astype(jnp.bfloat16),
        "norm_bias": noise(arg_keys[9], (L, 2, D), 0.3, 2.0, ((2, 8),)),
        "layer_scale": jnp.clip(jnp.exp(math.log(1.5) - 1.0986123 * jax.random.uniform(arg_keys[10], (L, 2, D), jnp.float32) ** levels(arg_keys[10], (L, 2, D), ((2, 8),), -0.2, 0.2)), 0.5, 1.5).astype(jnp.bfloat16),
        "out_bias": noise(arg_keys[11], (L, 2, D), 0.3, 2.0, ((2, 8),)),
    }


HIGH = lax.Precision.HIGHEST
EPS = 1e-06

@jax.custom_vjp
def low(v):
    return lax.optimization_barrier(v.astype(jnp.bfloat16)).astype(jnp.float32)

@jax.custom_vjp
def low_back(v):
    return v

def low_keep(v):
    return (low(v), None)

def low_pass(kept, grad):
    return (grad,)

def back_keep(v):
    return (v, None)

def back_low(kept, grad):
    return (low(grad),)
low.defvjp(low_keep, low_pass)
low_back.defvjp(back_keep, back_low)

def matmul(left, right):
    return jnp.dot(left, right, precision=HIGH)

def layer_norm(stream, gain, shift):
    centre = stream - lax.optimization_barrier(jnp.mean(stream, axis=-1, keepdims=True))
    inverse = lax.rsqrt(lax.optimization_barrier(jnp.mean(centre * centre, axis=-1, keepdims=True)) + EPS)
    return centre * inverse * gain + shift

def attend_image(packed):
    queries = packed[..., :HD]
    keys = packed[..., HD:2 * HD]
    values = packed[..., 2 * HD:]
    scores = jnp.einsum('qhd,khd->hqk', queries, keys, precision=HIGH) * HD ** (-0.5)
    scores = low_back(scores)
    probs = jax.nn.softmax(scores, axis=-1)
    return jnp.einsum('hqk,khd->qhd', low(probs), values, precision=HIGH)

def forward(stream, w_qkv, qv_bias, w_out, w_fc1, fc1_bias, w_fc2, norm_gain, norm_bias, layer_scale, out_bias):
    images = stream.shape[0] // SEQ
    for layer_index in range(L):
        normed = low(layer_norm(stream, norm_gain[layer_index, 0], norm_bias[layer_index, 0]))
        head_bias = qv_bias[layer_index]
        shift = jnp.concatenate([head_bias[:, :HD], jnp.zeros((H, HD), jnp.float32), head_bias[:, HD:]], axis=1).reshape(-1)
        projected = low_back(matmul(normed, w_qkv[layer_index].reshape(D, 3 * D)) + shift)
        projected = low(projected).reshape(images, SEQ, H, 3 * HD)
        mixed = lax.map(jax.checkpoint(attend_image), projected)
        mixed = low(low_back(mixed.reshape(-1, D)))
        attn_branch = low_back(matmul(mixed, w_out[layer_index].reshape(D, D))) + out_bias[layer_index, 0]
        stream = stream + layer_scale[layer_index, 0] * attn_branch
        normed_two = low(layer_norm(stream, norm_gain[layer_index, 1], norm_bias[layer_index, 1]))
        hidden_pre = low_back(matmul(normed_two, w_fc1[layer_index]) + fc1_bias[layer_index])
        hidden = low(jax.nn.gelu(hidden_pre, approximate=False))
        mlp_branch = low_back(matmul(hidden, w_fc2[layer_index])) + out_bias[layer_index, 1]
        stream = stream + layer_scale[layer_index, 1] * mlp_branch
    return stream

def reference(tokens, cotangent, w_qkv, qv_bias, w_out, w_fc1, fc1_bias, w_fc2, norm_gain, norm_bias, layer_scale, out_bias):
    inputs = (tokens, w_qkv, qv_bias, w_out, w_fc1, fc1_bias, w_fc2, norm_gain, norm_bias, layer_scale, out_bias)
    widened = [item.astype(jnp.float32) for item in inputs]
    output, pullback = jax.vjp(forward, *widened)
    grads = pullback(cotangent.astype(jnp.float32))
    return (output.astype(jnp.bfloat16), grads[0], grads[1], grads[2], grads[3], grads[4], grads[5], grads[6], grads[7], grads[8], grads[9], grads[10])
```

```python
import functools

import jax
import jax.numpy as jnp
from jax import lax
from jax.experimental import pallas as pl
from jax.experimental.pallas import tpu as pltpu
from jax.sharding import Mesh
from jax.sharding import PartitionSpec as P

D = 1024
HD = 64
SEQ = 1024
ROWS = 128
NX = 4
NF = 8
NZ = 2
F32 = jnp.float32
BF = jnp.bfloat16
TENSOR = ("tensor_0", "tensor_1", "tensor_2")
FSDP_TENSOR = ("fsdp", "tensor_0", "tensor_1", "tensor_2")
MESH = pl.DeviceIdType.MESH
EPS = 1e-06
ROOT_HALF = 0.7071067811865476
INV_ROOT_TAU = 0.3989422804014327
HALF = ROWS // 2
TOP = pl.ds(0, HALF)
BOTTOM = pl.ds(HALF, HALF)
VMEM_BYTES = 56 * 1024 * 1024
OWN, LEFT, RIGHT, FAR = 0, 1, 2, 3


def dot_nn(left, right):
    return lax.dot_general(left, right, (((1,), (0,)), ((), ())), preferred_element_type=F32)


def dot_nt(left, right):
    return lax.dot_general(left, right, (((1,), (1,)), ((), ())), preferred_element_type=F32)


def dot_tn(left, right):
    return lax.dot_general(left, right, (((0,), (0,)), ((), ())), preferred_element_type=F32)


def norm_parts(stream):
    centre = stream - jnp.mean(stream, axis=-1, keepdims=True)
    inverse = lax.rsqrt(jnp.mean(centre * centre, axis=-1, keepdims=True) + EPS)
    return centre * inverse, inverse


def norm_backward(grad_out, normal, inverse, gain):
    scaled = grad_out * gain
    return inverse * (
        scaled
        - jnp.mean(scaled, axis=-1, keepdims=True)
        - normal * jnp.mean(scaled * normal, axis=-1, keepdims=True)
    )


def group_index():
    return lax.axis_index("fsdp"), lax.axis_index("tensor_1")


def group_peer(step):
    f, z = group_index()
    at = lax.rem(f * NZ + z + step, NF * NZ)
    return at // NZ, lax.rem(at, NZ)


def group_id(step):
    f, z = group_peer(step)
    return {"fsdp": f, "tensor_1": z}


def cols(f, width=128):
    return pl.ds(pl.multiple_of(f * width, width), width)


VIEWS = {
    "qkv": lambda ref, f, z: ref.at[:, z, :, cols(f)],
    "out": lambda ref, f, z: ref.at[z, :, cols(f)],
    "small": lambda ref, f, z: ref.at[z, :, cols(f)],
    "fc1": lambda ref, f, z: ref.at[cols(f), cols(z, 256)],
    "fc2": lambda ref, f, z: ref.at[cols(z, 256), cols(f)],
    "vec": lambda ref, f, z: ref.at[:, cols(f)],
    "unit": lambda ref, f, z: ref.at[z],
}


class Gather:
    def __init__(self, kinds, srcs, dsts, send, recv):
        self.jobs = list(zip(kinds, srcs, dsts))
        self.send, self.recv = send, recv

    def copy(self, i, step):
        kind, src, dst = self.jobs[i]
        f, z = group_index()
        return pltpu.make_async_remote_copy(
            src_ref=src,
            dst_ref=VIEWS[kind](dst, f, z),
            send_sem=self.send.at[i, step],
            recv_sem=self.recv.at[i, step],
            device_id=group_id(step),
            device_id_type=MESH,
        )

    def start(self):
        for i in range(len(self.jobs)):
            self.local(i).start()
            lax.fori_loop(1, NF * NZ, lambda s, _: (self.copy(i, s).start(), 0)[1], 0)

    def local(self, i):
        kind, src, dst = self.jobs[i]
        f, z = group_index()
        return pltpu.make_async_copy(src, VIEWS[kind](dst, f, z), self.send.at[i, 0])

    def wait(self):
        for i in range(len(self.jobs)):
            self.local(i).wait()
            lax.fori_loop(1, NF * NZ, lambda s, _: (self.copy(i, s).wait(), 0)[1], 0)


class Scatter:
    def __init__(self, kinds, srcs, lands, outs, send, recv):
        self.jobs = list(zip(kinds, srcs, lands, outs))
        self.send, self.recv = send, recv

    def copy(self, i, step):
        kind, src, land, _ = self.jobs[i]
        f, z = group_peer(step)
        return pltpu.make_async_remote_copy(
            src_ref=VIEWS[kind](src, f, z),
            dst_ref=land.at[step],
            send_sem=self.send.at[i, step],
            recv_sem=self.recv.at[i, step],
            device_id=group_id(step),
            device_id_type=MESH,
        )

    def local(self, i):
        kind, src, land, _ = self.jobs[i]
        f, z = group_index()
        return pltpu.make_async_copy(VIEWS[kind](src, f, z), land.at[0], self.send.at[i, 0])

    def start(self):
        for i in range(len(self.jobs)):
            self.local(i).start()
            lax.fori_loop(1, NF * NZ, lambda s, _: (self.copy(i, s).start(), 0)[1], 0)

    def finish(self):
        for i, (_, _, land, out) in enumerate(self.jobs):
            self.local(i).wait()
            lax.fori_loop(1, NF * NZ, lambda s, _: (self.copy(i, s).wait(), 0)[1], 0)
            total = land[0].astype(F32)
            for s in range(1, NF * NZ):
                total = total + land[s].astype(F32)
            out[...] = total


def greet(ring, group, whole_ring=False):
    barrier = pltpu.get_barrier_semaphore()
    count = 0

    def signal(where):
        pl.semaphore_signal(barrier, inc=1, device_id=where, device_id_type=MESH)

    if ring:
        x, c = lax.axis_index("tensor_0"), lax.axis_index("tensor_2")
        signal({"tensor_2": 1 - c})
        signal({"tensor_0": lax.rem(x + 1, NX)})
        signal({"tensor_0": lax.rem(x + 3, NX)})
        count += 3
    if whole_ring:
        for s in range(1, 2 * NX):
            signal(ring_id(s))
        count += 2 * NX - 1
    if group and NF * NZ > 1:
        lax.fori_loop(1, NF * NZ, lambda s, _: (signal(group_id(s)), 0)[1], 0)
        count += NF * NZ - 1
    pl.semaphore_wait(barrier, count)


def ring_id(step):
    x, c = lax.axis_index("tensor_0"), lax.axis_index("tensor_2")
    at = lax.rem(x * 2 + c + step, 2 * NX)
    return {"tensor_0": at // 2, "tensor_2": lax.rem(at, 2)}


class Ring:
    def __init__(self, gath, part, pin, sout, rin, held, gsend, grecv, ssend, srecv):
        self.x, self.c = lax.axis_index("tensor_0"), lax.axis_index("tensor_2")
        self.at = [self.x] + [lax.rem(self.x + s, NX) for s in (3, 1, 2)]
        self.gath, self.part, self.pin = gath, part, pin
        self.sout, self.rin, self.held = sout, rin, held
        self.gsend, self.grecv, self.ssend, self.srecv = gsend, grecv, ssend, srecv
        self.left = {"tensor_0": self.at[LEFT]}
        self.right = {"tensor_0": self.at[RIGHT]}
        self.twin = {"tensor_2": 1 - self.c}

    def gcopy(self, i):
        who, rows, to = (
            (OWN, None, self.twin),
            (OWN, TOP, self.right),
            (OWN, BOTTOM, self.right),
            (OWN, BOTTOM, self.left),
            (OWN, TOP, self.left),
            (LEFT, TOP, self.right),
            (RIGHT, BOTTOM, self.left),
            (LEFT, None, self.twin),
            (RIGHT, None, self.twin),
            (FAR, TOP, self.twin),
            (FAR, BOTTOM, self.twin),
        )[i]
        ref = self.gath.at[self.at[who], self.c]
        if rows is not None:
            ref = ref.at[rows]
        return pltpu.make_async_remote_copy(
            src_ref=ref,
            dst_ref=ref,
            send_sem=self.gsend.at[i],
            recv_sem=self.grecv.at[i],
            device_id=to,
            device_id_type=MESH,
        )

    def set_own(self, rows):
        self.gath[self.x, self.c] = rows
        for i in (1, 3, 2, 4, 0):
            self.gcopy(i).start()

    def arrive(self, who):
        def got(i):
            self.gcopy(i).wait_recv()

        def go(i):
            self.gcopy(i).start()

        if who == OWN:
            got(0)
        elif who == LEFT:
            got(1), go(5), got(3), go(6), got(2), go(7), got(4), go(8), got(7)
        elif who == RIGHT:
            got(8)
        else:
            got(5), go(9), got(6), go(10), got(9), got(10)

    def rows(self, who):
        return self.gath[self.at[who]].reshape(2 * ROWS, D)

    def pcopy(self, who):
        return pltpu.make_async_remote_copy(
            src_ref=self.part.at[who, 1 - self.c],
            dst_ref=self.pin.at[who],
            send_sem=self.ssend.at[6 + who],
            recv_sem=self.srecv.at[6 + who],
            device_id=self.twin,
            device_id_type=MESH,
        )

    def scopy(self, i):
        return pltpu.make_async_remote_copy(
            src_ref=self.sout.at[i],
            dst_ref=self.rin.at[i],
            send_sem=self.ssend.at[i],
            recv_sem=self.srecv.at[i],
            device_id=self.left if i in (1, 4, 5) else self.right,
            device_id_type=MESH,
        )

    def put(self, who, value):
        self.part[who] = value.astype(BF).reshape(2, ROWS, D)
        self.pcopy(who).start()

    def send(self, i, value):
        self.sout[i] = value.astype(BF)
        self.scopy(i).start()

    def flush(self, who):
        self.pcopy(who).wait_recv()
        total = self.part[who, self.c].astype(F32) + self.pin[who].astype(F32)
        if who == FAR:
            self.send(0, total[:HALF])
            self.send(1, total[HALF:])
        elif who == RIGHT:
            self.send(2, total[HALF:])
            self.held[0] = total[:HALF]
        elif who == LEFT:
            self.send(4, total[:HALF])
            self.held[1] = total[HALF:]

    def merge(self):
        self.scopy(0).wait_recv()
        self.send(3, self.held[0] + self.rin[0].astype(F32))
        self.scopy(1).wait_recv()
        self.send(5, self.held[1] + self.rin[1].astype(F32))

    def finish(self):
        self.pcopy(OWN).wait_recv()
        total = self.part[OWN, self.c].astype(F32) + self.pin[OWN].astype(F32)
        for i in (2, 4, 3, 5):
            self.scopy(i).wait_recv()
        top = total[:HALF] + self.rin[3].astype(F32) + self.rin[4].astype(F32)
        bottom = total[HALF:] + self.rin[2].astype(F32) + self.rin[5].astype(F32)
        return jnp.concatenate([top, bottom], axis=0)

    def drain(self):
        for i in range(11):
            self.gcopy(i).wait_send()
        for i in range(6):
            self.scopy(i).wait_send()
        for i in range(4):
            self.pcopy(i).wait_send()


RING_SCRATCH = [
    pltpu.VMEM((NX, 2, ROWS, D), BF),
    pltpu.VMEM((NX, ROWS, D), BF),
    pltpu.VMEM((6, HALF, D), BF),
    pltpu.VMEM((6, HALF, D), BF),
    pltpu.VMEM((2, HALF, D), F32),
    pltpu.SemaphoreType.DMA((11,)),
    pltpu.SemaphoreType.DMA((11,)),
    pltpu.SemaphoreType.DMA((10,)),
    pltpu.SemaphoreType.DMA((10,)),
]
GATH = pltpu.VMEM((NX, 2, ROWS, D), BF)


def job_sems(count):
    return [pltpu.SemaphoreType.DMA((count, NF * NZ))] * 2


FULL = {
    "qkv": (3, NZ, HD, D),
    "out": (NZ, HD, D),
    "small": (NZ, 16, D),
    "fc1": (D, 512),
    "fc2": (512, D),
    "vec": (16, D),
    "unit": (NZ, 8, 128),
}
PIECE = {
    "qkv": (3, HD, 128),
    "out": (HD, 128),
    "small": (16, 128),
    "fc1": (128, 256),
    "fc2": (256, 128),
    "vec": (16, 128),
    "unit": (8, 128),
}
VM = pl.BlockSpec(memory_space=pltpu.VMEM)


def shaped(shape, dtype=F32):
    return jax.ShapeDtypeStruct(shape, dtype)


def call(body, outs, scratch, ident, args):
    return pl.pallas_call(
        body,
        out_shape=outs,
        in_specs=[VM] * len(args),
        out_specs=[VM] * len(outs),
        scratch_shapes=scratch,
        compiler_params=pltpu.CompilerParams(
            collective_id=ident, has_side_effects=True, vmem_limit_bytes=VMEM_BYTES
        ),
    )(*args)


def first_kernel(qkv, out, small0, small1, qkv_o, out_o, small0_o, small1_o, gs, gr):
    greet(False, True)
    job = Gather(
        ("small", "small", "qkv", "out"),
        (small0, small1, qkv, out),
        (small0_o, small1_o, qkv_o, out_o),
        gs,
        gr,
    )
    job.start()
    job.wait()


def lane_head(shape):
    return lax.broadcasted_iota(jnp.int32, shape, len(shape) - 1) // HD


def attn_forward(
    stream, small, wqkv, wout, fc1, fc2, mid_o, branch_o, normed_o, q_o, k_o, v_o, mixed_o, lse_o,
    fc1_o, fc2_o, masked, vt, mixt, *rest
):
    ring = Ring(normed_o, *rest[:9])
    greet(True, True)
    job = Gather(("fc1", "fc2"), (fc1, fc2), (fc1_o, fc2_o), *rest[9:])
    vec = small[0]
    normal, _ = norm_parts(stream[...])
    ring.set_own((normal * vec[0:1] + vec[2:3]).astype(BF))
    job.start()
    weights = wqkv[...].reshape(3 * 2 * HD, D)
    bias_a, bias_b = small[0, 10:11, 0:128], small[1, 10:11, 0:128]
    shift = jnp.concatenate(
        [
            bias_a[:, :HD],
            bias_b[:, :HD],
            jnp.zeros((1, 128), F32),
            bias_a[:, HD:],
            bias_b[:, HD:],
        ],
        axis=1,
    )
    for who in (OWN, LEFT, RIGHT, FAR):
        ring.arrive(who)
        at = ring.at[who]
        qkv = (dot_nt(ring.rows(who), weights) + shift).astype(BF)
        keys, values = qkv[:, 128:256], qkv[:, 256:]
        q_o[at] = qkv[:, :128] * 0.125
        k_o[at] = keys
        v_o[at] = values
        head = lane_head((2 * ROWS, 128))
        for h in range(2):
            masked[h, at] = jnp.where(head == h, keys, jnp.zeros_like(keys))
        vt[at] = values.astype(F32).T.astype(BF)
    for step, who in enumerate((FAR, LEFT, RIGHT, OWN)):
        at = ring.at[who]
        queries = q_o[at]

        def head_step(h, _, queries=queries, at=at):
            scores = dot_nt(masked[h].reshape(SEQ, 128), queries)
            highest = jnp.max(scores, axis=0, keepdims=True)
            weights = jnp.exp(scores - highest)
            total = jnp.sum(weights, axis=0, keepdims=True)
            probs = (weights * (1.0 / total)).astype(BF)
            span = pl.ds(pl.multiple_of(h * HD, HD), HD)
            mixed = jnp.zeros((HD, 2 * ROWS), F32)
            for part in range(NX):
                mixed = mixed + dot_nn(
                    vt[part, span, :], probs[part * 2 * ROWS : (part + 1) * 2 * ROWS]
                )
            mixt[span, :] = mixed
            lse_o[at, h] = highest + jnp.log(total)
            return 0

        lax.fori_loop(0, 2, head_step, 0)
        mixed = mixt[...].T.astype(BF)
        mixed_o[at] = mixed
        ring.put(who, dot_nn(mixed, wout[...].reshape(2 * HD, D)))
        if who == LEFT:
            ring.flush(FAR)
        elif who == RIGHT:
            ring.flush(LEFT)
            ring.flush(RIGHT)
            ring.merge()
    branch = ring.finish() + vec[6:7]
    branch_o[...] = branch
    mid_o[...] = stream[...] + vec[4:5] * branch
    job.wait()
    ring.drain()


def mlp_forward(with_job, *refs):
    refs = list(refs)
    mid, small, fc1, fc2 = refs[:4]
    del refs[:4]
    kinds = ("qkv", "out") if with_job else ()
    srcs = [refs.pop(0) for _ in kinds]
    out_o, branch_o, normed_o, hidden_o, slope_o = refs[:5]
    del refs[:5]
    dsts = [refs.pop(0) for _ in kinds]
    ring = Ring(normed_o, *refs[:9])
    greet(True, with_job)
    vec = small[0]
    normal, _ = norm_parts(mid[...])
    ring.set_own((normal * vec[1:2] + vec[3:4]).astype(BF))
    if with_job:
        job = Gather(kinds, srcs, dsts, *refs[9:])
        job.start()
    bias = jnp.concatenate([small[z, r : r + 1, 0:128] for z in range(NZ) for r in (8, 9)], axis=1)
    for who in (OWN, LEFT, RIGHT, FAR):
        ring.arrive(who)
        at = ring.at[who]
        pre = dot_nn(ring.rows(who), fc1[...]) + bias
        phi = 0.5 * (1.0 + lax.erf(pre * ROOT_HALF))
        hidden = (pre * phi).astype(BF)
        slope_o[at] = (phi + pre * INV_ROOT_TAU * jnp.exp(-0.5 * pre * pre)).astype(BF)
        hidden_o[at] = hidden
        ring.put(who, dot_nn(hidden, fc2[...]))
        if who == RIGHT:
            ring.flush(LEFT)
            ring.flush(RIGHT)
    ring.flush(FAR)
    ring.merge()
    branch = ring.finish() + vec[7:8]
    branch_o[...] = branch
    out_o[...] = mid[...] + vec[5:6] * branch
    if with_job:
        job.wait()
    ring.drain()


def row_sum(value):
    return jnp.sum(value, axis=0, keepdims=True)


def mlp_backward(with_job, *refs):
    refs = list(refs)
    grad, branch, mid, small, fc1, fc2, normed, hidden, slope = refs[:9]
    del refs[:9]
    kinds = ("qkv", "out") if with_job else ()
    srcs = [refs.pop(0) for _ in kinds]
    grad_o, dfc1_o, dfc2_o, sums_o = refs[:4]
    del refs[:4]
    outs = [refs.pop(0) for _ in kinds]
    gath, pre = refs[:2]
    del refs[:2]
    ring = Ring(gath, *refs[:9])
    del refs[:9]
    greet(True, with_job)
    vec = small[0]
    g = grad[...]
    scaled = vec[5:6] * g
    ring.set_own(scaled.astype(BF))
    if with_job:
        job = Scatter(kinds, srcs, refs[:2], outs, *refs[2:])
        job.start()
    sums_o[...] = jnp.zeros((8, D), F32)
    sums_o[2:3, :] = row_sum(branch[...] * g)
    sums_o[3:4, :] = row_sum(scaled)
    unit = jnp.zeros((1, 512), F32)
    for who in (OWN, LEFT, RIGHT, FAR):
        ring.arrive(who)
        at = ring.at[who]
        back = (dot_nt(ring.rows(who), fc2[...]) * slope[at].astype(F32)).astype(BF)
        pre[at] = back
        unit = unit + row_sum(back.astype(F32))
        ring.put(who, dot_nt(back, fc1[...]))
        if who == RIGHT:
            ring.flush(LEFT)
            ring.flush(RIGHT)
    ring.flush(FAR)
    sums_o[4:5, 0:512] = unit
    dfc2_o[...] = dot_tn(hidden[...].reshape(SEQ, 512), gath[...].reshape(SEQ, D)).astype(BF)
    ring.merge()
    dfc1_o[...] = dot_tn(normed[...].reshape(SEQ, D), pre[...].reshape(SEQ, 512)).astype(BF)
    back = ring.finish()
    normal, inverse = norm_parts(mid[...])
    sums_o[0:1, :] = row_sum(back * normal)
    sums_o[1:2, :] = row_sum(back)
    grad_o[...] = g + norm_backward(back, normal, inverse, vec[1:2])
    if with_job:
        job.finish()
    ring.drain()


def attn_backward(
    grad, branch, stream, small, wqkv, wout, normed, q, k, v, mixed, lse, dfc1, dfc2,
    grad_o, dqkv_o, dout_o, sums_o, gfc1_o, gfc2_o,
    gath, mk, mv, kt, dq, dqt, dk, dv, dall, gmix, *rest
):
    ring = Ring(gath, *rest[:9])
    greet(True, True)
    vec = small[0]
    g = grad[...]
    scaled = vec[4:5] * g
    ring.set_own(scaled.astype(BF))
    job = Scatter(("fc1", "fc2"), (dfc1, dfc2), rest[9:11], (gfc1_o, gfc2_o), *rest[11:])
    job.start()
    sums_o[...] = jnp.zeros((8, D), F32)
    sums_o[2:3, :] = row_sum(branch[...] * g)
    sums_o[3:4, :] = row_sum(scaled)
    head = lane_head((2 * ROWS, 128))
    for part in range(NX):
        for h in range(2):
            mk[h, part] = jnp.where(head == h, k[part], jnp.zeros_like(k[part]))
            mv[h, part] = jnp.where(head == h, v[part], jnp.zeros_like(v[part]))
        kt[part] = k[part].astype(F32).T.astype(BF)
    dk[...] = jnp.zeros((SEQ, 128), F32)
    dv[...] = jnp.zeros((SEQ, 128), F32)
    out_weights = wout[...].reshape(2 * HD, D)
    for who in (OWN, LEFT, RIGHT, FAR):
        ring.arrive(who)
        at = ring.at[who]
        gm = dot_nt(ring.rows(who), out_weights).astype(BF)
        gmix[at] = gm

        def head_step(h, _, at=at):
            queries = q[at]
            mine = gmix[at]
            probs = jnp.exp(dot_nt(mk[h].reshape(SEQ, 128), queries) - lse[at, h])
            back = dot_nt(mv[h].reshape(SEQ, 128), mine)
            delta = jnp.sum(probs * back, axis=0, keepdims=True)
            dscores = (probs * (back - delta)).astype(BF)
            span = pl.ds(pl.multiple_of(h * HD, HD), HD)
            turned = jnp.zeros((HD, 2 * ROWS), F32)
            for part in range(NX):
                turned = turned + dot_nn(
                    kt[part, span, :], dscores[part * 2 * ROWS : (part + 1) * 2 * ROWS]
                )
            dqt[span, :] = turned * 0.125
            mask = head == h
            dk[...] += dot_nn(dscores, jnp.where(mask, queries, jnp.zeros_like(queries)))
            dv[...] += dot_nn(probs.astype(BF), jnp.where(mask, mine, jnp.zeros_like(mine)))
            return 0

        lax.fori_loop(0, 2, head_step, 0)
        dq[at] = dqt[...].T.astype(BF)
    for part in range(NX):
        span = slice(part * 2 * ROWS, (part + 1) * 2 * ROWS)
        dall[part] = jnp.concatenate(
            [dq[part], dk[span, :].astype(BF), dv[span, :].astype(BF)], axis=1
        )
    weights = wqkv[...].reshape(3 * 2 * HD, D)
    for who in (FAR, LEFT, RIGHT, OWN):
        ring.put(who, dot_nn(dall[ring.at[who]], weights))
        if who == LEFT:
            ring.flush(FAR)
        elif who == RIGHT:
            ring.flush(LEFT)
            ring.flush(RIGHT)
    dout_o[...] = dot_tn(
        mixed[...].reshape(SEQ, 128), gath[...].reshape(SEQ, D)
    ).astype(BF).reshape(NZ, HD, D)
    ring.merge()
    whole = dall[...].reshape(SEQ, 384)
    dqkv_o[...] = dot_tn(whole, normed[...].reshape(SEQ, D)).astype(BF).reshape(3, NZ, HD, D)
    unit = row_sum(whole.astype(F32))
    sums_o[4:5, 0:256] = jnp.concatenate(
        [unit[:, 0:HD], unit[:, 256 : 256 + HD], unit[:, HD:128], unit[:, 256 + HD : 384]], axis=1
    )
    back = ring.finish()
    normal, inverse = norm_parts(stream[...])
    sums_o[0:1, :] = row_sum(back * normal)
    sums_o[1:2, :] = row_sum(back)
    grad_o[...] = g + norm_backward(back, normal, inverse, vec[0:1])
    job.finish()
    ring.drain()


def last_kernel(
    dqkv, dout, s00, s01, s10, s11, gqkv_o, gout_o, vec_o, unit_o,
    vec_src, unit_src, vec_sum, land_q, land_o, land_v, land_u, ring_land, gs, gr, rs, rr
):
    greet(False, True, True)
    for layer, pair in enumerate(((s00, s01), (s10, s11))):
        for i, ref in enumerate(pair):
            for kind in range(4):
                row = kind * 4 + layer * 2 + i
                vec_src[row : row + 1, :] = ref[kind : kind + 1, :]
        for z in range(NZ):
            for r in range(2):
                at = z * 256 + r * 128
                row = layer * 2 + r
                unit_src[z, row : row + 1, :] = pair[1][4:5, at : at + 128]
            row = 4 + layer
            unit_src[z, row : row + 1, :] = pair[0][4:5, z * 128 : (z + 1) * 128]
            row = 6 + layer
            unit_src[z, row : row + 1, :] = jnp.zeros((1, 128), F32)
    job = Scatter(
        ("vec", "unit", "qkv", "out"),
        (vec_src, unit_src, dqkv, dout),
        (land_v, land_u, land_q, land_o),
        (vec_sum, unit_o, gqkv_o, gout_o),
        gs,
        gr,
    )
    job.start()
    job.finish()

    def copy(step):
        return pltpu.make_async_remote_copy(
            src_ref=vec_sum,
            dst_ref=ring_land.at[step],
            send_sem=rs.at[step],
            recv_sem=rr.at[step],
            device_id=ring_id(step),
            device_id_type=MESH,
        )

    for s in range(1, 2 * NX):
        copy(s).start()
    for s in range(1, 2 * NX):
        copy(s).wait()
    total = vec_sum[...]
    for s in range(1, 2 * NX):
        total = total + ring_land[s]
    vec_o[...] = total


def row_arrays():
    return [shaped((ROWS, D)), shaped((ROWS, D))]


def run_first(qkv, out, small0, small1):
    outs = [
        shaped(FULL["qkv"], BF),
        shaped(FULL["out"], BF),
        shaped(FULL["small"]),
        shaped(FULL["small"]),
    ]
    return call(first_kernel, outs, job_sems(4), 1, (qkv, out, small0, small1))


def run_attn_forward(stream, small, wqkv, wout, fc1, fc2):
    heads = shaped((NX, 2 * ROWS, 128), BF)
    outs = row_arrays() + [
        shaped((NX, 2, ROWS, D), BF),
        heads,
        heads,
        heads,
        heads,
        shaped((NX, 2, 1, 2 * ROWS)),
        shaped(FULL["fc1"], BF),
        shaped(FULL["fc2"], BF),
    ]
    scratch = [
        pltpu.VMEM((2, NX, 2 * ROWS, 128), BF),
        pltpu.VMEM((NX, 128, 2 * ROWS), BF),
        pltpu.VMEM((128, 2 * ROWS), F32),
        *RING_SCRATCH,
        *job_sems(2),
    ]
    return call(attn_forward, outs, scratch, 2, (stream, small, wqkv, wout, fc1, fc2))


def run_mlp_forward(mid, small, fc1, fc2, following):
    units = shaped((NX, 2 * ROWS, 512), BF)
    outs = row_arrays() + [shaped((NX, 2, ROWS, D), BF), units, units]
    scratch = list(RING_SCRATCH)
    if following:
        outs += [shaped(FULL["qkv"], BF), shaped(FULL["out"], BF)]
        scratch += job_sems(2)
    body = functools.partial(mlp_forward, bool(following))
    return call(body, outs, scratch, 3 if following else 4, (mid, small, fc1, fc2, *following))


def landing(kind, dtype=BF):
    return pltpu.VMEM((NF * NZ, *PIECE[kind]), dtype)


def run_mlp_backward(args, following):
    outs = [
        shaped((ROWS, D)),
        shaped(FULL["fc1"], BF),
        shaped(FULL["fc2"], BF),
        shaped((8, D)),
    ]
    scratch = [GATH, pltpu.VMEM((NX, 2 * ROWS, 512), BF), *RING_SCRATCH]
    if following:
        outs += [shaped(PIECE["qkv"]), shaped(PIECE["out"])]
        scratch += [landing("qkv"), landing("out"), *job_sems(2)]
    body = functools.partial(mlp_backward, bool(following))
    return call(body, outs, scratch, 6 if following else 5, (*args, *following))


def run_attn_backward(*args):
    outs = [
        shaped((ROWS, D)),
        shaped(FULL["qkv"], BF),
        shaped(FULL["out"], BF),
        shaped((8, D)),
        shaped(PIECE["fc1"]),
        shaped(PIECE["fc2"]),
    ]
    heads = pltpu.VMEM((NX, 2 * ROWS, 128), BF)
    scratch = [
        GATH,
        pltpu.VMEM((2, NX, 2 * ROWS, 128), BF),
        pltpu.VMEM((2, NX, 2 * ROWS, 128), BF),
        pltpu.VMEM((NX, 128, 2 * ROWS), BF),
        heads,
        pltpu.VMEM((128, 2 * ROWS), F32),
        pltpu.VMEM((SEQ, 128), F32),
        pltpu.VMEM((SEQ, 128), F32),
        pltpu.VMEM((NX, 2 * ROWS, 384), BF),
        heads,
        *RING_SCRATCH,
        landing("fc1"),
        landing("fc2"),
        *job_sems(2),
    ]
    return call(attn_backward, outs, scratch, 7, args)


def run_last(dqkv, dout, sums):
    outs = [
        shaped(PIECE["qkv"]),
        shaped(PIECE["out"]),
        shaped(PIECE["vec"]),
        shaped(PIECE["unit"]),
    ]
    scratch = [
        pltpu.VMEM(FULL["vec"], F32),
        pltpu.VMEM(FULL["unit"], F32),
        pltpu.VMEM(PIECE["vec"], F32),
        landing("qkv"),
        landing("out"),
        landing("vec", F32),
        landing("unit", F32),
        pltpu.VMEM((2 * NX, *PIECE["vec"]), F32),
        *job_sems(4),
        pltpu.SemaphoreType.DMA((2 * NX,)),
        pltpu.SemaphoreType.DMA((2 * NX,)),
    ]
    return call(last_kernel, outs, scratch, 8, (dqkv, dout, *sums))


def swapped(rows):
    if NZ == 1:
        return rows
    pairs = []
    for x in range(NX):
        for z in range(NZ):
            to = (x + 2, 0) if x < 2 and z == 1 else (x - 2, 1) if x >= 2 and z == 0 else (x, z)
            pairs.append((x * NZ + z, to[0] * NZ + to[1]))
    return lax.ppermute(rows, ("tensor_0", "tensor_1"), pairs)


def on_device(
    tokens,
    cotangent,
    w_qkv,
    qv_bias,
    w_out,
    w_fc1,
    fc1_bias,
    w_fc2,
    norm_gain,
    norm_bias,
    layer_scale,
    out_bias,
):
    layers = range(w_qkv.shape[0])
    small = []
    for l in layers:
        rows = [a[l].astype(F32) for a in (norm_gain, norm_bias, layer_scale, out_bias)]
        rows.append(fc1_bias[l].astype(F32).reshape(2, 128))
        rows.append(qv_bias[l].astype(F32))
        rows.append(jnp.zeros((5, 128), F32))
        small.append(jnp.concatenate(rows, axis=0))
    qkv_shards = [w_qkv[l][:, 0, :].T.reshape(3, HD, 128) for l in layers]
    out_shards = [w_out[l][0] for l in layers]
    stream = swapped(tokens).astype(F32)
    grad = swapped(cotangent).astype(F32)
    wqkv, wout, *smalls = run_first(qkv_shards[0], out_shards[0], *small)
    kept = []
    for l in layers:
        mid, branch, normed, q, k, v, mixed, lse, fc1, fc2 = run_attn_forward(
            stream, smalls[l], wqkv, wout, w_fc1[l], w_fc2[l]
        )
        following = (qkv_shards[1], out_shards[1]) if l == 0 else ()
        out, branch_two, normed_two, hidden, slope, *more = run_mlp_forward(
            mid, smalls[l], fc1, fc2, following
        )
        kept.append(
            (
                (branch_two, mid, smalls[l], fc1, fc2, normed_two, hidden, slope),
                (branch, stream, smalls[l], wqkv, wout, normed, q, k, v, mixed, lse),
            )
        )
        stream = out
        if more:
            wqkv, wout = more
    out_tokens = swapped(stream.astype(BF))
    matrices = {}
    sums = {}
    pending = ()
    for l in reversed(layers):
        two, one = kept[l]
        grad, dfc1, dfc2, sums[l, 1], *more = run_mlp_backward((grad, *two), pending)
        if more:
            matrices[l + 1, "qkv"], matrices[l + 1, "out"] = more
        grad, dqkv, dout, sums[l, 0], matrices[l, "fc1"], matrices[l, "fc2"] = run_attn_backward(
            grad, *one, dfc1, dfc2
        )
        pending = (dqkv, dout)
    matrices[0, "qkv"], matrices[0, "out"], vec, unit = run_last(
        *pending, (sums[0, 0], sums[0, 1], sums[1, 0], sums[1, 1])
    )
    vec = vec.reshape(4, 2, 2, 128)

    def both(kind):
        return jnp.stack([matrices[l, kind] for l in layers])

    grad_w_qkv = jnp.swapaxes(both("qkv").reshape(2, 3 * HD, 128), 1, 2)[:, :, None, :]
    return (
        out_tokens,
        swapped(grad),
        grad_w_qkv,
        unit[4:6][:, None, :],
        both("out")[:, None],
        both("fc1"),
        unit[0:4].reshape(2, 256),
        both("fc2"),
        vec[0],
        vec[1],
        vec[2],
        vec[3],
    )


def solution(mesh):
    split = Mesh(
        mesh.devices.reshape(mesh.shape["fsdp"], NX, NZ, 2),
        ("fsdp", "tensor_0", "tensor_1", "tensor_2"),
    )
    return jax.shard_map(
        on_device,
        mesh=split,
        in_specs=(
            P(FSDP_TENSOR, None),
            P(FSDP_TENSOR, None),
            P(None, "fsdp", TENSOR, None),
            P(None, TENSOR, None),
            P(None, TENSOR, None, "fsdp"),
            P(None, "fsdp", TENSOR),
            P(None, TENSOR),
            P(None, TENSOR, "fsdp"),
            P(None, None, "fsdp"),
            P(None, None, "fsdp"),
            P(None, None, "fsdp"),
            P(None, None, "fsdp"),
        ),
        out_specs=(
            P(FSDP_TENSOR, None),
            P(FSDP_TENSOR, None),
            P(None, "fsdp", TENSOR, None),
            P(None, TENSOR, None),
            P(None, TENSOR, None, "fsdp"),
            P(None, "fsdp", TENSOR),
            P(None, TENSOR),
            P(None, TENSOR, "fsdp"),
            P(None, None, "fsdp"),
            P(None, None, "fsdp"),
            P(None, None, "fsdp"),
            P(None, None, "fsdp"),
        ),
        check_vma=False,
    )
```

```python
import jax
import jax.numpy as jnp
from jax import lax
from jax.experimental import pallas as pl
from jax.experimental.pallas import tpu as pltpu
from jax.sharding import Mesh
from jax.sharding import PartitionSpec as P

D = 1024
HD = 64
SEQ = 1024
ROWS = 128
NX = 4
NF = 8
NZ = 2
F32 = jnp.float32
BF = jnp.bfloat16
TENSOR = ("tensor_0", "tensor_1", "tensor_2")
FSDP_TENSOR = ("fsdp", "tensor_0", "tensor_1", "tensor_2")
MESH = pl.DeviceIdType.MESH
EPS = 1e-06
ROOT_HALF = 0.7071067811865476
INV_ROOT_TAU = 0.3989422804014327
HALF = ROWS // 2
TOP = pl.ds(0, HALF)
BOTTOM = pl.ds(HALF, HALF)
VMEM_BYTES = 60 * 1024 * 1024
OWN, LEFT, RIGHT, FAR = 0, 1, 2, 3


def dot_nn(left, right):
    return lax.dot_general(left, right, (((1,), (0,)), ((), ())), preferred_element_type=F32)


def dot_nt(left, right):
    return lax.dot_general(left, right, (((1,), (1,)), ((), ())), preferred_element_type=F32)


def dot_tn(left, right):
    return lax.dot_general(left, right, (((0,), (0,)), ((), ())), preferred_element_type=F32)


def norm_parts(stream):
    centre = stream - jnp.mean(stream, axis=-1, keepdims=True)
    inverse = lax.rsqrt(jnp.mean(centre * centre, axis=-1, keepdims=True) + EPS)
    return centre * inverse, inverse


def norm_backward(grad_out, normal, inverse, gain):
    scaled = grad_out * gain
    return inverse * (
        scaled
        - jnp.mean(scaled, axis=-1, keepdims=True)
        - normal * jnp.mean(scaled * normal, axis=-1, keepdims=True)
    )


def group_index():
    return lax.axis_index("fsdp"), lax.axis_index("tensor_1")


def group_peer(step):
    f, z = group_index()
    at = lax.rem(f * NZ + z + step, NF * NZ)
    return at // NZ, lax.rem(at, NZ)


def group_id(step):
    f, z = group_peer(step)
    return {"fsdp": f, "tensor_1": z}


def cols(f, width=128):
    return pl.ds(pl.multiple_of(f * width, width), width)


VIEWS = {
    "qkv": lambda ref, f, z: ref.at[:, z, :, cols(f)],
    "out": lambda ref, f, z: ref.at[z, :, cols(f)],
    "small": lambda ref, f, z: ref.at[z, :, :, cols(f)],
    "fc1": lambda ref, f, z: ref.at[cols(f), cols(z, 256)],
    "fc2": lambda ref, f, z: ref.at[cols(z, 256), cols(f)],
    "vec": lambda ref, f, z: ref.at[:, cols(f)],
    "unit": lambda ref, f, z: ref.at[z],
}


def each_peer(act):
    def step(s, _):
        act(s)
        return 0

    lax.fori_loop(1, NF * NZ, step, 0)


class Gather:
    def __init__(self, kind, src, dst, send, recv):
        self.view, self.src, self.dst = VIEWS[kind], src, dst
        self.send, self.recv = send, recv

    def copy(self, step):
        return pltpu.make_async_remote_copy(
            src_ref=self.src,
            dst_ref=self.view(self.dst, *group_index()),
            send_sem=self.send.at[step],
            recv_sem=self.recv.at[step],
            device_id=group_id(step),
            device_id_type=MESH,
        )

    def local(self):
        return pltpu.make_async_copy(
            self.src, self.view(self.dst, *group_index()), self.send.at[0]
        )

    def start(self):
        self.local().start()
        each_peer(lambda s: self.copy(s).start())

    def wait(self):
        self.local().wait()
        each_peer(lambda s: self.copy(s).wait())


class Scatter:
    def __init__(self, kind, src, land, send, recv):
        self.view, self.src, self.land = VIEWS[kind], src, land
        self.send, self.recv = send, recv

    def copy(self, step):
        return pltpu.make_async_remote_copy(
            src_ref=self.view(self.src, *group_peer(step)),
            dst_ref=self.land.at[step],
            send_sem=self.send.at[step],
            recv_sem=self.recv.at[step],
            device_id=group_id(step),
            device_id_type=MESH,
        )

    def local(self):
        return pltpu.make_async_copy(
            self.view(self.src, *group_index()), self.land.at[0], self.send.at[0]
        )

    def start(self):
        self.local().start()
        each_peer(lambda s: self.copy(s).start())

    def total(self):
        self.local().wait()
        each_peer(lambda s: self.copy(s).wait())
        return sum(self.land[s].astype(F32) for s in range(NF * NZ))


class Swap:
    def __init__(self, src, dst, send, recv):
        x, z = lax.axis_index("tensor_0"), lax.axis_index("tensor_1")
        self.moves = lax.rem(x // 2 + z, 2) == 1
        self.remote = pltpu.make_async_remote_copy(
            src_ref=src,
            dst_ref=dst,
            send_sem=send,
            recv_sem=recv,
            device_id=swap_id(),
            device_id_type=MESH,
        )
        self.stay = pltpu.make_async_copy(src, dst, send)

    def start(self):
        pl.when(self.moves)(self.remote.start)
        pl.when(jnp.logical_not(self.moves))(self.stay.start)

    def wait(self):
        pl.when(self.moves)(self.remote.wait)
        pl.when(jnp.logical_not(self.moves))(self.stay.wait)


def swap_id():
    x, z = lax.axis_index("tensor_0"), lax.axis_index("tensor_1")
    return {"tensor_0": lax.rem(x + 2, NX), "tensor_1": 1 - z}


def ring_id(step):
    x, c = lax.axis_index("tensor_0"), lax.axis_index("tensor_2")
    at = lax.rem(x * 2 + c + step, 2 * NX)
    return {"tensor_0": at // 2, "tensor_2": lax.rem(at, 2)}


def greet():
    barrier = pltpu.get_barrier_semaphore()

    def signal(where):
        pl.semaphore_signal(barrier, inc=1, device_id=where, device_id_type=MESH)

    for s in range(1, 2 * NX):
        signal(ring_id(s))
    signal(swap_id())
    each_peer(lambda s: signal(group_id(s)))
    return lambda: pl.semaphore_wait(barrier, 2 * NX + NF * NZ - 1)


class Ring:
    def __init__(self, part, pin, sout, rin, held, gsend, grecv, ssend, srecv):
        self.x, self.c = lax.axis_index("tensor_0"), lax.axis_index("tensor_2")
        self.at = [self.x] + [lax.rem(self.x + s, NX) for s in (3, 1, 2)]
        self.part, self.pin = part, pin
        self.sout, self.rin, self.held = sout, rin, held
        self.gsend, self.grecv, self.ssend, self.srecv = gsend, grecv, ssend, srecv
        self.left = {"tensor_0": self.at[LEFT]}
        self.right = {"tensor_0": self.at[RIGHT]}
        self.twin = {"tensor_2": 1 - self.c}

    def gcopy(self, i):
        who, rows, to = (
            (OWN, None, self.twin),
            (OWN, TOP, self.right),
            (OWN, BOTTOM, self.right),
            (OWN, BOTTOM, self.left),
            (OWN, TOP, self.left),
            (LEFT, TOP, self.right),
            (RIGHT, BOTTOM, self.left),
            (LEFT, None, self.twin),
            (RIGHT, None, self.twin),
            (FAR, TOP, self.twin),
            (FAR, BOTTOM, self.twin),
        )[i]
        ref = self.gath.at[self.at[who], self.c]
        if rows is not None:
            ref = ref.at[rows]
        return pltpu.make_async_remote_copy(
            src_ref=ref,
            dst_ref=ref,
            send_sem=self.gsend.at[i],
            recv_sem=self.grecv.at[i],
            device_id=to,
            device_id_type=MESH,
        )

    def set_own(self, gath, rows):
        self.gath = gath
        self.gath[self.x, self.c] = rows
        for i in (1, 3, 2, 4, 0):
            self.gcopy(i).start()

    def arrive(self, who):
        def got(i):
            self.gcopy(i).wait_recv()

        def go(i):
            self.gcopy(i).start()

        if who == OWN:
            got(0)
        elif who == LEFT:
            got(1), go(5), got(3), go(6), got(2), go(7), got(4), go(8), got(7)
        elif who == RIGHT:
            got(8)
        else:
            got(5), go(9), got(6), go(10), got(9), got(10)

    def rows(self, who):
        return self.gath[self.at[who]].reshape(2 * ROWS, D)

    def pcopy(self, who):
        return pltpu.make_async_remote_copy(
            src_ref=self.part.at[who, 1 - self.c],
            dst_ref=self.pin.at[who],
            send_sem=self.ssend.at[6 + who],
            recv_sem=self.srecv.at[6 + who],
            device_id=self.twin,
            device_id_type=MESH,
        )

    def scopy(self, i):
        return pltpu.make_async_remote_copy(
            src_ref=self.sout.at[i],
            dst_ref=self.rin.at[i],
            send_sem=self.ssend.at[i],
            recv_sem=self.srecv.at[i],
            device_id=self.left if i in (1, 4, 5) else self.right,
            device_id_type=MESH,
        )

    def put(self, who, value):
        self.part[who] = value.astype(BF).reshape(2, ROWS, D)
        self.pcopy(who).start()

    def send(self, i, value):
        self.sout[i] = value.astype(BF)
        self.scopy(i).start()

    def flush(self, who):
        self.pcopy(who).wait_recv()
        total = self.part[who, self.c].astype(F32) + self.pin[who].astype(F32)
        if who == FAR:
            self.send(0, total[:HALF])
            self.send(1, total[HALF:])
        elif who == RIGHT:
            self.send(2, total[HALF:])
            self.held[0] = total[:HALF]
        elif who == LEFT:
            self.send(4, total[:HALF])
            self.held[1] = total[HALF:]

    def merge(self):
        self.scopy(0).wait_recv()
        self.send(3, self.held[0] + self.rin[0].astype(F32))
        self.scopy(1).wait_recv()
        self.send(5, self.held[1] + self.rin[1].astype(F32))

    def finish(self):
        self.pcopy(OWN).wait_recv()
        total = self.part[OWN, self.c].astype(F32) + self.pin[OWN].astype(F32)
        for i in (2, 4, 3, 5):
            self.scopy(i).wait_recv()
        top = total[:HALF] + self.rin[3].astype(F32) + self.rin[4].astype(F32)
        bottom = total[HALF:] + self.rin[2].astype(F32) + self.rin[5].astype(F32)
        return jnp.concatenate([top, bottom], axis=0)

    def drain(self):
        for i in range(11):
            self.gcopy(i).wait_send()
        for i in range(6):
            self.scopy(i).wait_send()
        for i in range(4):
            self.pcopy(i).wait_send()


RING_SCRATCH = [
    pltpu.VMEM((NX, 2, ROWS, D), BF),
    pltpu.VMEM((NX, ROWS, D), BF),
    pltpu.VMEM((6, HALF, D), BF),
    pltpu.VMEM((6, HALF, D), BF),
    pltpu.VMEM((2, HALF, D), F32),
    pltpu.SemaphoreType.DMA((11,)),
    pltpu.SemaphoreType.DMA((11,)),
    pltpu.SemaphoreType.DMA((10,)),
    pltpu.SemaphoreType.DMA((10,)),
]

def lane_head(shape):
    return lax.broadcasted_iota(jnp.int32, shape, len(shape) - 1) // HD


def row_sum(value):
    return jnp.sum(value, axis=0, keepdims=True)


PIECE = {
    "qkv": (3, HD, 128),
    "out": (HD, 128),
    "fc1": (128, 256),
    "fc2": (256, 128),
    "vec": (16, 128),
    "unit": (8, 128),
}
HEADS = (NX, 2 * ROWS, 128)


def sems(*shape):
    return [pltpu.SemaphoreType.DMA(shape)] * 2


SCRATCH = dict(
    small_src=pltpu.VMEM((2, 16, 128), F32),
    small=pltpu.VMEM((NZ, 2, 16, D), F32),
    qkv_src=pltpu.VMEM((2, 3, HD, 128), BF),
    wqkv=pltpu.VMEM((2, 3, NZ, HD, D), BF),
    wout=pltpu.VMEM((2, NZ, HD, D), BF),
    wfc1=pltpu.VMEM((2, D, 512), BF),
    wfc2=pltpu.VMEM((2, 512, D), BF),
    start=pltpu.VMEM((ROWS, D), BF),
    first_grad=pltpu.VMEM((ROWS, D), BF),
    ending=pltpu.VMEM((ROWS, D), BF),
    stream=pltpu.VMEM((3, ROWS, D), F32),
    mid=pltpu.VMEM((2, ROWS, D), F32),
    branch=pltpu.VMEM((2, 2, ROWS, D), F32),
    grad=pltpu.VMEM((ROWS, D), F32),
    normed=pltpu.VMEM((2, 2, NX, 2, ROWS, D), BF),
    q=pltpu.VMEM((2, *HEADS), BF),
    k=pltpu.VMEM((2, *HEADS), BF),
    v=pltpu.VMEM((2, *HEADS), BF),
    mixed=pltpu.VMEM((2, *HEADS), BF),
    lse=pltpu.VMEM((2, NX, 2, 1, 2 * ROWS), F32),
    hidden=pltpu.VMEM((2, NX, 2 * ROWS, 512), BF),
    slope=pltpu.VMEM((2, NX, 2 * ROWS, 512), BF),
    mk=pltpu.VMEM((2, *HEADS), BF),
    mv=pltpu.VMEM((2, *HEADS), BF),
    turned=pltpu.VMEM((NX, 128, 2 * ROWS), BF),
    mixt=pltpu.VMEM((128, 2 * ROWS), F32),
    gath=pltpu.VMEM((2, NX, 2, ROWS, D), BF),
    pre=pltpu.VMEM((NX, 2 * ROWS, 512), BF),
    gmix=pltpu.VMEM(HEADS, BF),
    dq=pltpu.VMEM(HEADS, BF),
    dk=pltpu.VMEM((SEQ, 128), F32),
    dv=pltpu.VMEM((SEQ, 128), F32),
    dall=pltpu.VMEM((NX, 2 * ROWS, 384), BF),
    sums=pltpu.VMEM((2, 2, 8, D), F32),
    dqkv=pltpu.VMEM((3, NZ, HD, D), BF),
    dout=pltpu.VMEM((NZ, HD, D), BF),
    dfc1=pltpu.VMEM((D, 512), BF),
    dfc2=pltpu.VMEM((512, D), BF),
    vec_src=pltpu.VMEM((16, D), F32),
    unit_src=pltpu.VMEM((NZ, 8, 128), F32),
    vec_sum=pltpu.VMEM((16, 128), F32),
    land_qkv=pltpu.VMEM((2, NF * NZ, *PIECE["qkv"]), BF),
    land_out=pltpu.VMEM((2, NF * NZ, *PIECE["out"]), BF),
    land_fc1=pltpu.VMEM((2, NF * NZ, *PIECE["fc1"]), BF),
    land_fc2=pltpu.VMEM((2, NF * NZ, *PIECE["fc2"]), BF),
    land_vec=pltpu.VMEM((NF * NZ, *PIECE["vec"]), F32),
    land_unit=pltpu.VMEM((NF * NZ, *PIECE["unit"]), F32),
    land_ring=pltpu.VMEM((2 * NX, *PIECE["vec"]), F32),
    small_sems=sems(NF * NZ),
    qkv_sems=sems(2, NF * NZ),
    out_sems=sems(2, NF * NZ),
    fc1_sems=sems(2, NF * NZ),
    fc2_sems=sems(2, NF * NZ),
    dqkv_sems=sems(2, NF * NZ),
    dout_sems=sems(2, NF * NZ),
    dfc1_sems=sems(2, NF * NZ),
    dfc2_sems=sems(2, NF * NZ),
    vec_sems=sems(NF * NZ),
    unit_sems=sems(NF * NZ),
    swap_sems=sems(4),
    ring_sems=sems(2 * NX),
    ring=RING_SCRATCH,
)


def scratch_list():
    flat = []
    for item in SCRATCH.values():
        flat += item if isinstance(item, list) else [item]
    return flat


class Refs:
    def __init__(self, flat):
        flat = list(flat)
        for name, item in SCRATCH.items():
            if isinstance(item, list):
                setattr(self, name, [flat.pop(0) for _ in item])
            else:
                setattr(self, name, flat.pop(0))


IN = ("tokens", "cotangent", "w_qkv", "qv_bias", "w_out", "w_fc1", "fc1_bias", "w_fc2")
IN += ("norm_gain", "norm_bias", "layer_scale", "out_bias")
OUT = ("out_tokens", "grad_tokens", "g_qkv", "g_out", "g_fc1", "g_fc2", "g_vec", "g_unit")


def pair(send_recv, *at):
    return [s.at[at] for s in send_recv]


class Program:
    def __init__(self, flat):
        for name, ref in zip(IN + OUT, flat):
            setattr(self, name, ref)
        self.r = Refs(flat[len(IN + OUT) :])
        self.ring = Ring(*self.r.ring)

    def small_job(self):
        r = self.r
        return Gather("small", r.small_src, r.small, *r.small_sems)

    def head_jobs(self, l):
        r = self.r
        return (
            Gather("qkv", r.qkv_src.at[l], r.wqkv.at[l], *pair(r.qkv_sems, l)),
            Gather("out", self.w_out.at[l], r.wout.at[l], *pair(r.out_sems, l)),
        )

    def unit_jobs(self, l):
        r = self.r
        return (
            Gather("fc1", self.w_fc1.at[l], r.wfc1.at[l], *pair(r.fc1_sems, l)),
            Gather("fc2", self.w_fc2.at[l], r.wfc2.at[l], *pair(r.fc2_sems, l)),
        )

    def head_sums(self, l):
        r = self.r
        return (
            Scatter("qkv", r.dqkv, r.land_qkv.at[l], *pair(r.dqkv_sems, l)),
            Scatter("out", r.dout, r.land_out.at[l], *pair(r.dout_sems, l)),
        )

    def unit_sums(self, l):
        r = self.r
        return (
            Scatter("fc1", r.dfc1, r.land_fc1.at[l], *pair(r.dfc1_sems, l)),
            Scatter("fc2", r.dfc2, r.land_fc2.at[l], *pair(r.dfc2_sems, l)),
        )

    def finish_heads(self, l):
        qkv, out = self.head_sums(l)
        self.g_qkv[l] = qkv.total().reshape(3 * HD, 128).T
        self.g_out[l] = out.total()

    def finish_units(self, l):
        fc1, fc2 = self.unit_sums(l)
        self.g_fc1[l] = fc1.total()
        self.g_fc2[l] = fc2.total()

    def swap(self, i, src, dst):
        return Swap(src, dst, *pair(self.r.swap_sems, i))

    def run(self):
        r = self.r
        greeted = greet()
        for l in range(2):
            at = 0
            for ref in (self.norm_gain, self.norm_bias, self.layer_scale, self.out_bias):
                r.small_src[l, at : at + 2, :] = ref[l].astype(F32)
                at += 2
            bias = self.fc1_bias[...].astype(F32)[l : l + 1]
            r.small_src[l, 8:9, :] = bias[:, :128]
            r.small_src[l, 9:10, :] = bias[:, 128:]
            r.small_src[l, 10:11, :] = self.qv_bias[...].astype(F32)[l : l + 1]
            r.small_src[l, 11:16, :] = jnp.zeros((5, 128), F32)
            turned = self.w_qkv[l].astype(F32).T.astype(BF)
            r.qkv_src[l] = turned.reshape(3, HD, 128)
        greeted()
        tokens = self.swap(0, self.tokens, r.start)
        cotangent = self.swap(1, self.cotangent, r.first_grad)
        tokens.start()
        self.small_job().start()
        for job in self.head_jobs(0):
            job.start()
        cotangent.start()
        tokens.wait()
        r.stream[0] = r.start[...].astype(F32)
        self.small_job().wait()
        lax.fori_loop(0, 2, self.forward, 0)
        r.ending[...] = r.stream[2].astype(BF)
        ending = self.swap(2, r.ending, self.out_tokens)
        ending.start()
        cotangent.wait()
        r.grad[...] = r.first_grad[...].astype(F32)
        lax.fori_loop(0, 2, self.backward, 0)
        back = self.swap(3, r.grad, self.grad_tokens)
        back.start()
        self.last_sums()
        ending.wait()
        back.wait()

    def forward(self, l, _):
        self.attn_forward(l)
        self.mlp_forward(l)
        return 0

    def backward(self, i, _):
        self.mlp_backward(1 - i)
        self.attn_backward(1 - i)
        return 0

    def attn_forward(self, l):
        r, ring = self.r, self.ring
        vec = r.small[0, l]
        normal, _ = norm_parts(r.stream[l])
        ring.set_own(r.normed.at[l, 0], (normal * vec[0:1] + vec[2:3]).astype(BF))
        bias_a, bias_b = r.small[0, l][10:11, 0:128], r.small[1, l][10:11, 0:128]
        shift = jnp.concatenate(
            [
                bias_a[:, :HD],
                bias_b[:, :HD],
                jnp.zeros((1, 128), F32),
                bias_a[:, HD:],
                bias_b[:, HD:],
            ],
            axis=1,
        )
        for job in self.head_jobs(l):
            job.wait()
        for job in self.unit_jobs(l):
            job.start()
        weights = r.wqkv[l].reshape(3 * 2 * HD, D)
        for who in (OWN, LEFT, RIGHT, FAR):
            ring.arrive(who)
            at = ring.at[who]
            qkv = (dot_nt(ring.rows(who), weights) + shift).astype(BF)
            keys, values = qkv[:, 128:256], qkv[:, 256:]
            r.q[l, at] = qkv[:, :128] * 0.125
            r.k[l, at] = keys
            r.v[l, at] = values
            head = lane_head((2 * ROWS, 128))
            for h in range(2):
                r.mk[h, at] = jnp.where(head == h, keys, jnp.zeros_like(keys))
            r.turned[at] = values.astype(F32).T.astype(BF)
        for who in (FAR, LEFT, RIGHT, OWN):
            at = ring.at[who]

            def head_step(h, _, at=at):
                scores = dot_nt(r.mk[h].reshape(SEQ, 128), r.q[l, at])
                highest = jnp.max(scores, axis=0, keepdims=True)
                weights = jnp.exp(scores - highest)
                total = jnp.sum(weights, axis=0, keepdims=True)
                probs = (weights * (1.0 / total)).astype(BF)
                span = pl.ds(pl.multiple_of(h * HD, HD), HD)
                mixed = jnp.zeros((HD, 2 * ROWS), F32)
                for part in range(NX):
                    mixed = mixed + dot_nn(
                        r.turned[part, span, :],
                        probs[part * 2 * ROWS : (part + 1) * 2 * ROWS],
                    )
                r.mixt[span, :] = mixed
                r.lse[l, at, h] = highest + jnp.log(total)
                return 0

            lax.fori_loop(0, 2, head_step, 0)
            mixed = r.mixt[...].T.astype(BF)
            r.mixed[l, at] = mixed
            ring.put(who, dot_nn(mixed, r.wout[l].reshape(2 * HD, D)))
            if who == LEFT:
                ring.flush(FAR)
            elif who == RIGHT:
                ring.flush(LEFT)
                ring.flush(RIGHT)
                ring.merge()
        branch = ring.finish() + vec[6:7]
        r.branch[l, 0] = branch
        r.mid[l] = r.stream[l] + vec[4:5] * branch
        ring.drain()

    def mlp_forward(self, l):
        r, ring = self.r, self.ring
        vec = r.small[0, l]
        normal, _ = norm_parts(r.mid[l])
        ring.set_own(r.normed.at[l, 1], (normal * vec[1:2] + vec[3:4]).astype(BF))
        bias = jnp.concatenate(
            [r.small[z, l][row : row + 1, 0:128] for z in range(NZ) for row in (8, 9)], axis=1
        )
        for job in self.unit_jobs(l):
            job.wait()

        @pl.when(l == 0)
        def _():
            for job in self.head_jobs(1):
                job.start()

        for who in (OWN, LEFT, RIGHT, FAR):
            ring.arrive(who)
            at = ring.at[who]
            pre = dot_nn(ring.rows(who), r.wfc1[l]) + bias
            phi = 0.5 * (1.0 + lax.erf(pre * ROOT_HALF))
            hidden = (pre * phi).astype(BF)
            slope = phi + pre * INV_ROOT_TAU * jnp.exp(-0.5 * pre * pre)
            r.slope[l, at] = slope.astype(BF)
            r.hidden[l, at] = hidden
            ring.put(who, dot_nn(hidden, r.wfc2[l]))
            if who == RIGHT:
                ring.flush(LEFT)
                ring.flush(RIGHT)
        ring.flush(FAR)
        ring.merge()
        branch = ring.finish() + vec[7:8]
        r.branch[l, 1] = branch
        r.stream[l + 1] = r.mid[l] + vec[5:6] * branch
        ring.drain()

    def begin_backward(self, l, i, gath):
        r = self.r
        g = r.grad[...]
        scaled = r.small[0, l][4 + i : 5 + i] * g
        self.ring.set_own(gath, scaled.astype(BF))
        r.sums[l, i] = jnp.zeros((8, D), F32)
        r.sums[l, i, 2:3, :] = row_sum(r.branch[l, i] * g)
        r.sums[l, i, 3:4, :] = row_sum(scaled)

    def end_backward(self, l, i, stream):
        r = self.r
        back = self.ring.finish()
        normal, inverse = norm_parts(stream)
        r.sums[l, i, 0:1, :] = row_sum(back * normal)
        r.sums[l, i, 1:2, :] = row_sum(back)
        gain = r.small[0, l][i : i + 1]
        r.grad[...] += norm_backward(back, normal, inverse, gain)
        self.ring.drain()

    def mlp_backward(self, l):
        r, ring = self.r, self.ring
        gath = r.gath.at[0]
        self.begin_backward(l, 1, gath)
        unit = jnp.zeros((1, 512), F32)
        for who in (OWN, LEFT, RIGHT, FAR):
            ring.arrive(who)
            at = ring.at[who]
            back = dot_nt(ring.rows(who), r.wfc2[l]) * r.slope[l, at].astype(F32)
            back = back.astype(BF)
            r.pre[at] = back
            unit = unit + row_sum(back.astype(F32))
            ring.put(who, dot_nt(back, r.wfc1[l]))
            if who == RIGHT:
                ring.flush(LEFT)
                ring.flush(RIGHT)
        ring.flush(FAR)
        r.sums[l, 1, 4:5, 0:512] = unit
        fc1, fc2 = self.unit_sums(l)
        r.dfc2[...] = dot_tn(
            r.hidden[l].reshape(SEQ, 512), gath[...].reshape(SEQ, D)
        ).astype(BF)
        fc2.start()
        ring.merge()
        r.dfc1[...] = dot_tn(
            r.normed[l, 1].reshape(SEQ, D), r.pre[...].reshape(SEQ, 512)
        ).astype(BF)
        fc1.start()

        @pl.when(l == 0)
        def _():
            self.finish_heads(1)

        self.end_backward(l, 1, r.mid[l])

    def attn_backward(self, l):
        r, ring = self.r, self.ring
        gath = r.gath.at[1]
        self.begin_backward(l, 0, gath)
        head = lane_head((2 * ROWS, 128))
        for part in range(NX):
            keys, values = r.k[l, part], r.v[l, part]
            for h in range(2):
                r.mk[h, part] = jnp.where(head == h, keys, jnp.zeros_like(keys))
                r.mv[h, part] = jnp.where(head == h, values, jnp.zeros_like(values))
            r.turned[part] = keys.astype(F32).T.astype(BF)
        r.dk[...] = jnp.zeros((SEQ, 128), F32)
        r.dv[...] = jnp.zeros((SEQ, 128), F32)
        for who in (OWN, LEFT, RIGHT, FAR):
            ring.arrive(who)
            at = ring.at[who]
            r.gmix[at] = dot_nt(ring.rows(who), r.wout[l].reshape(2 * HD, D)).astype(BF)

            def head_step(h, _, at=at):
                queries, mine = r.q[l, at], r.gmix[at]
                probs = jnp.exp(dot_nt(r.mk[h].reshape(SEQ, 128), queries) - r.lse[l, at, h])
                back = dot_nt(r.mv[h].reshape(SEQ, 128), mine)
                delta = jnp.sum(probs * back, axis=0, keepdims=True)
                dscores = (probs * (back - delta)).astype(BF)
                span = pl.ds(pl.multiple_of(h * HD, HD), HD)
                turned = jnp.zeros((HD, 2 * ROWS), F32)
                for part in range(NX):
                    turned = turned + dot_nn(
                        r.turned[part, span, :],
                        dscores[part * 2 * ROWS : (part + 1) * 2 * ROWS],
                    )
                r.mixt[span, :] = turned * 0.125
                mask = head == h
                r.dk[...] += dot_nn(dscores, jnp.where(mask, queries, jnp.zeros_like(queries)))
                r.dv[...] += dot_nn(
                    probs.astype(BF), jnp.where(mask, mine, jnp.zeros_like(mine))
                )
                return 0

            lax.fori_loop(0, 2, head_step, 0)
            r.dq[at] = r.mixt[...].T.astype(BF)
        for part in range(NX):
            span = slice(part * 2 * ROWS, (part + 1) * 2 * ROWS)
            r.dall[part] = jnp.concatenate(
                [r.dq[part], r.dk[span, :].astype(BF), r.dv[span, :].astype(BF)], axis=1
            )
        weights = r.wqkv[l].reshape(3 * 2 * HD, D)
        for who in (FAR, LEFT, RIGHT, OWN):
            ring.put(who, dot_nn(r.dall[ring.at[who]], weights))
            if who == LEFT:
                ring.flush(FAR)
            elif who == RIGHT:
                ring.flush(LEFT)
                ring.flush(RIGHT)
        qkv, out = self.head_sums(l)
        whole = r.dall[...].reshape(SEQ, 384)
        dqkv = dot_tn(whole, r.normed[l, 0].reshape(SEQ, D)).astype(BF)
        r.dqkv[...] = dqkv.reshape(3, NZ, HD, D)
        qkv.start()
        ring.merge()
        dout = dot_tn(r.mixed[l].reshape(SEQ, 128), gath[...].reshape(SEQ, D)).astype(BF)
        r.dout[...] = dout.reshape(NZ, HD, D)
        out.start()
        unit = row_sum(whole.astype(F32))
        r.sums[l, 0, 4:5, 0:256] = jnp.concatenate(
            [
                unit[:, 0:HD],
                unit[:, 256 : 256 + HD],
                unit[:, HD:128],
                unit[:, 256 + HD : 384],
            ],
            axis=1,
        )
        self.finish_units(l)
        self.end_backward(l, 0, r.stream[l])

    def last_sums(self):
        r = self.r
        for l in range(2):
            for i in range(2):
                sums = r.sums[l, i]
                for kind in range(4):
                    row = kind * 4 + l * 2 + i
                    r.vec_src[row : row + 1, :] = sums[kind : kind + 1]
            heads, units = r.sums[l, 0], r.sums[l, 1]
            for z in range(NZ):
                for at, row in ((0, l * 2), (128, l * 2 + 1)):
                    at = at + z * 256
                    r.unit_src[z, row : row + 1, :] = units[4:5, at : at + 128]
                r.unit_src[z, 4 + l : 5 + l, :] = heads[4:5, z * 128 : (z + 1) * 128]
                r.unit_src[z, 6 + l : 7 + l, :] = jnp.zeros((1, 128), F32)
        vec = Scatter("vec", r.vec_src, r.land_vec, *r.vec_sems)
        unit = Scatter("unit", r.unit_src, r.land_unit, *r.unit_sems)
        vec.start()
        unit.start()
        r.vec_sum[...] = vec.total()

        def copy(step):
            return pltpu.make_async_remote_copy(
                src_ref=r.vec_sum,
                dst_ref=r.land_ring.at[step],
                send_sem=r.ring_sems[0].at[step],
                recv_sem=r.ring_sems[1].at[step],
                device_id=ring_id(step),
                device_id_type=MESH,
            )

        for s in range(1, 2 * NX):
            copy(s).start()
        self.g_unit[...] = unit.total()
        self.finish_heads(0)
        total = r.vec_sum[...]
        for s in range(1, 2 * NX):
            copy(s).wait()
            total = total + r.land_ring[s]
        self.g_vec[...] = total


def whole_kernel(*flat):
    Program(flat).run()


def run_whole(*args):
    outs = [
        jax.ShapeDtypeStruct((ROWS, D), BF),
        jax.ShapeDtypeStruct((ROWS, D), F32),
        jax.ShapeDtypeStruct((2, 128, 3 * HD), F32),
        jax.ShapeDtypeStruct((2, HD, 128), F32),
        jax.ShapeDtypeStruct((2, 128, 256), F32),
        jax.ShapeDtypeStruct((2, 256, 128), F32),
        jax.ShapeDtypeStruct((16, 128), F32),
        jax.ShapeDtypeStruct((8, 128), F32),
    ]
    whole = pl.BlockSpec(memory_space=pltpu.VMEM)
    return pl.pallas_call(
        whole_kernel,
        out_shape=outs,
        in_specs=[whole] * len(args),
        out_specs=[whole] * len(outs),
        scratch_shapes=scratch_list(),
        compiler_params=pltpu.CompilerParams(
            collective_id=0, has_side_effects=True, vmem_limit_bytes=VMEM_BYTES
        ),
        cost_estimate=pl.CostEstimate(
            flops=24_000_000_000, bytes_accessed=8_000_000, transcendentals=10_000_000
        ),
    )(*args)


def on_device(
    tokens,
    cotangent,
    w_qkv,
    qv_bias,
    w_out,
    w_fc1,
    fc1_bias,
    w_fc2,
    norm_gain,
    norm_bias,
    layer_scale,
    out_bias,
):
    out_tokens, grad_tokens, g_qkv, g_out, g_fc1, g_fc2, g_vec, g_unit = run_whole(
        tokens,
        cotangent,
        w_qkv.reshape(2, 128, 3 * HD),
        qv_bias.reshape(2, 128),
        w_out.reshape(2, HD, 128),
        w_fc1,
        fc1_bias,
        w_fc2,
        norm_gain,
        norm_bias,
        layer_scale,
        out_bias,
    )
    vec = g_vec.reshape(4, 2, 2, 128)
    return (
        out_tokens,
        grad_tokens,
        g_qkv[:, :, None, :],
        g_unit[4:6][:, None, :],
        g_out[:, None],
        g_fc1,
        g_unit[0:4].reshape(2, 256),
        g_fc2,
        vec[0],
        vec[1],
        vec[2],
        vec[3],
    )


def solution(mesh):
    split = Mesh(
        mesh.devices.reshape(mesh.shape["fsdp"], NX, NZ, 2),
        ("fsdp", "tensor_0", "tensor_1", "tensor_2"),
    )
    return jax.shard_map(
        on_device,
        mesh=split,
        in_specs=(
            P(FSDP_TENSOR, None),
            P(FSDP_TENSOR, None),
            P(None, "fsdp", TENSOR, None),
            P(None, TENSOR, None),
            P(None, TENSOR, None, "fsdp"),
            P(None, "fsdp", TENSOR),
            P(None, TENSOR),
            P(None, TENSOR, "fsdp"),
            P(None, None, "fsdp"),
            P(None, None, "fsdp"),
            P(None, None, "fsdp"),
            P(None, None, "fsdp"),
        ),
        out_specs=(
            P(FSDP_TENSOR, None),
            P(FSDP_TENSOR, None),
            P(None, "fsdp", TENSOR, None),
            P(None, TENSOR, None),
            P(None, TENSOR, None, "fsdp"),
            P(None, "fsdp", TENSOR),
            P(None, TENSOR),
            P(None, TENSOR, "fsdp"),
            P(None, None, "fsdp"),
            P(None, None, "fsdp"),
            P(None, None, "fsdp"),
            P(None, None, "fsdp"),
        ),
        check_vma=False,
    )
```

```python
import jax
import jax.numpy as jnp
from jax import lax
from jax.experimental import pallas as pl
from jax.experimental.pallas import tpu as pltpu
from jax.sharding import Mesh
from jax.sharding import PartitionSpec as P

D = 1024
HD = 64
SEQ = 1024
ROWS = 128
NX = 4
NF = 8
NZ = 2
F32 = jnp.float32
BF = jnp.bfloat16
TENSOR = ("tensor_0", "tensor_1", "tensor_2")
FSDP_TENSOR = ("fsdp", "tensor_0", "tensor_1", "tensor_2")
MESH = pl.DeviceIdType.MESH
EPS = 1e-06
ROOT_HALF = 0.7071067811865476
INV_ROOT_TAU = 0.3989422804014327
CHUNKS = 2
PART = ROWS // CHUNKS
HALF = PART // 2
GCOPIES = 10
SCOPIES = 10
TOP = pl.ds(0, HALF)
BOTTOM = pl.ds(HALF, HALF)
VMEM_BYTES = 60 * 1024 * 1024
OWN, LEFT, RIGHT, FAR = 0, 1, 2, 3


def dot_nn(left, right):
    return lax.dot_general(left, right, (((1,), (0,)), ((), ())), preferred_element_type=F32)


def dot_nt(left, right):
    return lax.dot_general(left, right, (((1,), (1,)), ((), ())), preferred_element_type=F32)


def dot_tn(left, right):
    return lax.dot_general(left, right, (((0,), (0,)), ((), ())), preferred_element_type=F32)


def norm_parts(stream):
    centre = stream - jnp.mean(stream, axis=-1, keepdims=True)
    inverse = lax.rsqrt(jnp.mean(centre * centre, axis=-1, keepdims=True) + EPS)
    return centre * inverse, inverse


def norm_backward(grad_out, normal, inverse, gain):
    scaled = grad_out * gain
    return inverse * (
        scaled
        - jnp.mean(scaled, axis=-1, keepdims=True)
        - normal * jnp.mean(scaled * normal, axis=-1, keepdims=True)
    )


def group_index():
    return lax.axis_index("fsdp"), lax.axis_index("tensor_1")


def group_peer(step):
    f, z = group_index()
    at = lax.rem(f * NZ + z + step, NF * NZ)
    return at // NZ, lax.rem(at, NZ)


def group_id(step):
    f, z = group_peer(step)
    return {"fsdp": f, "tensor_1": z}


def cols(f, width=128):
    return pl.ds(pl.multiple_of(f * width, width), width)


VIEWS = {
    "qkv": lambda ref, f, z: ref.at[:, z, :, cols(f)],
    "out": lambda ref, f, z: ref.at[z, :, cols(f)],
    "small": lambda ref, f, z: ref.at[z, :, :, cols(f)],
    "fc1": lambda ref, f, z: ref.at[cols(f), cols(z, 256)],
    "fc2": lambda ref, f, z: ref.at[cols(z, 256), cols(f)],
    "vec": lambda ref, f, z: ref.at[:, cols(f)],
    "unit": lambda ref, f, z: ref.at[z],
}


def each_peer(act):
    def step(s, _):
        act(s)
        return 0

    lax.fori_loop(1, NF * NZ, step, 0)


class Gather:
    def __init__(self, kind, src, dst, send, recv):
        self.view, self.src, self.dst = VIEWS[kind], src, dst
        self.send, self.recv = send, recv

    def copy(self, step):
        return pltpu.make_async_remote_copy(
            src_ref=self.src,
            dst_ref=self.view(self.dst, *group_index()),
            send_sem=self.send.at[step],
            recv_sem=self.recv.at[step],
            device_id=group_id(step),
            device_id_type=MESH,
        )

    def local(self):
        return pltpu.make_async_copy(
            self.src, self.view(self.dst, *group_index()), self.send.at[0]
        )

    def start(self):
        self.local().start()
        each_peer(lambda s: self.copy(s).start())

    def wait(self):
        self.local().wait()
        each_peer(lambda s: self.copy(s).wait())


class Scatter:
    def __init__(self, kind, src, land, send, recv):
        self.view, self.src, self.land = VIEWS[kind], src, land
        self.send, self.recv = send, recv

    def copy(self, step):
        return pltpu.make_async_remote_copy(
            src_ref=self.view(self.src, *group_peer(step)),
            dst_ref=self.land.at[step],
            send_sem=self.send.at[step],
            recv_sem=self.recv.at[step],
            device_id=group_id(step),
            device_id_type=MESH,
        )

    def local(self):
        return pltpu.make_async_copy(
            self.view(self.src, *group_index()), self.land.at[0], self.send.at[0]
        )

    def start(self):
        self.local().start()
        each_peer(lambda s: self.copy(s).start())

    def total(self):
        self.local().wait()
        each_peer(lambda s: self.copy(s).wait())
        return sum(self.land[s].astype(F32) for s in range(NF * NZ))


class Swap:
    def __init__(self, src, dst, send, recv):
        x, z = lax.axis_index("tensor_0"), lax.axis_index("tensor_1")
        self.moves = lax.rem(x // 2 + z, 2) == 1
        self.remote = pltpu.make_async_remote_copy(
            src_ref=src,
            dst_ref=dst,
            send_sem=send,
            recv_sem=recv,
            device_id=swap_id(),
            device_id_type=MESH,
        )
        self.stay = pltpu.make_async_copy(src, dst, send)

    def start(self):
        pl.when(self.moves)(self.remote.start)
        pl.when(jnp.logical_not(self.moves))(self.stay.start)

    def wait(self):
        pl.when(self.moves)(self.remote.wait)
        pl.when(jnp.logical_not(self.moves))(self.stay.wait)


def swap_id():
    x, z = lax.axis_index("tensor_0"), lax.axis_index("tensor_1")
    return {"tensor_0": lax.rem(x + 2, NX), "tensor_1": 1 - z}


def ring_id(step):
    x, c = lax.axis_index("tensor_0"), lax.axis_index("tensor_2")
    at = lax.rem(x * 2 + c + step, 2 * NX)
    return {"tensor_0": at // 2, "tensor_2": lax.rem(at, 2)}


def greet():
    barrier = pltpu.get_barrier_semaphore()

    def signal(where):
        pl.semaphore_signal(barrier, inc=1, device_id=where, device_id_type=MESH)

    for s in range(1, 2 * NX):
        signal(ring_id(s))
    signal(swap_id())
    each_peer(lambda s: signal(group_id(s)))
    return lambda: pl.semaphore_wait(barrier, 2 * NX + NF * NZ - 1)


class Ring:
    def __init__(self, part, pin, sout, rin, held, gsend, grecv, ssend, srecv):
        self.x, self.c = lax.axis_index("tensor_0"), lax.axis_index("tensor_2")
        self.at = [self.x] + [lax.rem(self.x + s, NX) for s in (3, 1, 2)]
        self.part, self.pin = part, pin
        self.sout, self.rin, self.held = sout, rin, held
        self.gsend, self.grecv, self.ssend, self.srecv = gsend, grecv, ssend, srecv
        self.left = {"tensor_0": self.at[LEFT]}
        self.right = {"tensor_0": self.at[RIGHT]}
        self.twin = {"tensor_2": 1 - self.c}

    def gcopy(self, ch, i):
        who, rows, to = (
            (OWN, None, self.twin),
            (OWN, TOP, self.right),
            (OWN, BOTTOM, self.right),
            (OWN, BOTTOM, self.left),
            (OWN, TOP, self.left),
            (LEFT, TOP, self.right),
            (RIGHT, BOTTOM, self.left),
            (LEFT, None, self.twin),
            (RIGHT, None, self.twin),
            (FAR, None, self.twin),
        )[i]
        ref = self.gath.at[self.at[who], ch, self.c]
        if rows is not None:
            ref = ref.at[rows]
        return pltpu.make_async_remote_copy(
            src_ref=ref,
            dst_ref=ref,
            send_sem=self.gsend.at[ch * GCOPIES + i],
            recv_sem=self.grecv.at[ch * GCOPIES + i],
            device_id=to,
            device_id_type=MESH,
        )

    def got(self, ch, i):
        self.gcopy(ch, i).wait_recv()

    def go(self, ch, *which):
        for i in which:
            self.gcopy(ch, i).start()

    def set_own(self, gath, rows):
        self.gath = gath
        for ch in range(CHUNKS):
            gath[self.x, ch, self.c] = rows[ch * PART : (ch + 1) * PART]
        for ch in range(CHUNKS):
            self.go(ch, 1, 3, 2, 4, 0)

    def near(self, ch):
        self.got(ch, 1)
        self.go(ch, 5)
        self.got(ch, 3)
        self.go(ch, 6)
        self.got(ch, 2)
        self.go(ch, 7)
        self.got(ch, 4)
        self.go(ch, 8)

    def far(self, ch):
        self.got(ch, 5)
        self.got(ch, 6)
        self.go(ch, 9)

    def arrive(self, ch, who):
        self.got(ch, (0, 7, 8, 9)[who])

    def arrive_both(self, who):
        self.arrive(0, who)
        self.arrive(1, who)

    def chunk(self, ch, who):
        return self.gath[self.at[who], ch].reshape(2 * PART, D)

    def rows(self, who):
        return self.gath[self.at[who]].reshape(2 * ROWS, D)

    def pcopy(self, ch, who):
        return pltpu.make_async_remote_copy(
            src_ref=self.part.at[ch, who, 1 - self.c],
            dst_ref=self.pin.at[ch, who],
            send_sem=self.ssend.at[ch * SCOPIES + 6 + who],
            recv_sem=self.srecv.at[ch * SCOPIES + 6 + who],
            device_id=self.twin,
            device_id_type=MESH,
        )

    def scopy(self, ch, i):
        return pltpu.make_async_remote_copy(
            src_ref=self.sout.at[ch, i],
            dst_ref=self.rin.at[ch, i],
            send_sem=self.ssend.at[ch * SCOPIES + i],
            recv_sem=self.srecv.at[ch * SCOPIES + i],
            device_id=self.left if i in (1, 4, 5) else self.right,
            device_id_type=MESH,
        )

    def put(self, ch, who, value):
        self.part[ch, who] = value.astype(BF).reshape(2, PART, D)
        self.pcopy(ch, who).start()

    def put_both(self, who, value):
        self.put(0, who, value[: 2 * PART])
        self.put(1, who, value[2 * PART :])

    def send(self, ch, i, value):
        self.sout[ch, i] = value.astype(BF)
        self.scopy(ch, i).start()

    def both_cores(self, ch, who):
        self.pcopy(ch, who).wait_recv()
        return self.part[ch, who, self.c].astype(F32) + self.pin[ch, who].astype(F32)

    def flush(self, ch, who):
        total = self.both_cores(ch, who)
        if who == FAR:
            self.send(ch, 0, total[:HALF])
            self.send(ch, 1, total[HALF:])
        elif who == RIGHT:
            self.send(ch, 2, total[HALF:])
            self.held[ch, 0] = total[:HALF]
        else:
            self.send(ch, 4, total[:HALF])
            self.held[ch, 1] = total[HALF:]

    def flush_both(self, *which):
        for who in which:
            for ch in range(CHUNKS):
                self.flush(ch, who)

    def merge(self, ch):
        self.scopy(ch, 0).wait_recv()
        self.send(ch, 3, self.held[ch, 0] + self.rin[ch, 0].astype(F32))
        self.scopy(ch, 1).wait_recv()
        self.send(ch, 5, self.held[ch, 1] + self.rin[ch, 1].astype(F32))

    def finish(self):
        rows = []
        for ch in range(CHUNKS):
            total = self.both_cores(ch, OWN)
            for i in (2, 4, 3, 5):
                self.scopy(ch, i).wait_recv()
            rin = [self.rin[ch, i].astype(F32) for i in (2, 3, 4, 5)]
            rows += [total[:HALF] + rin[1] + rin[2], total[HALF:] + rin[0] + rin[3]]
        return jnp.concatenate(rows, axis=0)

    def drain(self):
        for ch in range(CHUNKS):
            for i in range(GCOPIES):
                self.gcopy(ch, i).wait_send()
            for i in range(6):
                self.scopy(ch, i).wait_send()
            for i in range(4):
                self.pcopy(ch, i).wait_send()

    def by_chunks(self, step):
        self.arrive(0, OWN)
        step(0, OWN)
        self.near(0)
        self.arrive(1, OWN)
        step(1, OWN)
        for who in (LEFT, RIGHT):
            self.arrive(0, who)
            step(0, who)
        self.near(1)
        self.flush(0, LEFT)
        self.flush(0, RIGHT)
        self.far(0)
        self.arrive(1, LEFT)
        step(1, LEFT)
        self.arrive(0, FAR)
        step(0, FAR)
        self.far(1)
        self.arrive(1, RIGHT)
        step(1, RIGHT)
        self.flush(0, FAR)
        self.arrive(1, FAR)
        step(1, FAR)
        self.flush(1, LEFT)
        self.flush(1, RIGHT)
        self.flush(1, FAR)
        self.merge(0)

    def by_blocks(self, step):
        self.arrive_both(OWN)
        step(OWN)
        self.near(0)
        self.near(1)
        self.arrive_both(LEFT)
        step(LEFT)
        self.far(0)
        self.far(1)
        self.arrive_both(RIGHT)
        step(RIGHT)
        self.arrive_both(FAR)
        step(FAR)

    def back_by_blocks(self, value):
        for who in (FAR, LEFT, RIGHT, OWN):
            self.put_both(who, value(who))
            if who == LEFT:
                self.flush_both(FAR)
            elif who == RIGHT:
                self.flush_both(LEFT, RIGHT)


RING_SCRATCH = [
    pltpu.VMEM((CHUNKS, NX, 2, PART, D), BF),
    pltpu.VMEM((CHUNKS, NX, PART, D), BF),
    pltpu.VMEM((CHUNKS, 6, HALF, D), BF),
    pltpu.VMEM((CHUNKS, 6, HALF, D), BF),
    pltpu.VMEM((CHUNKS, 2, HALF, D), F32),
    pltpu.SemaphoreType.DMA((CHUNKS * GCOPIES,)),
    pltpu.SemaphoreType.DMA((CHUNKS * GCOPIES,)),
    pltpu.SemaphoreType.DMA((CHUNKS * SCOPIES,)),
    pltpu.SemaphoreType.DMA((CHUNKS * SCOPIES,)),
]


def lane_head(shape):
    return lax.broadcasted_iota(jnp.int32, shape, len(shape) - 1) // HD


def row_sum(value):
    return jnp.sum(value, axis=0, keepdims=True)


PIECE = {
    "qkv": (3, HD, 128),
    "out": (HD, 128),
    "fc1": (128, 256),
    "fc2": (256, 128),
    "vec": (16, 128),
    "unit": (8, 128),
}
HEADS = (NX, 2 * ROWS, 128)


def sems(*shape):
    return [pltpu.SemaphoreType.DMA(shape)] * 2


SCRATCH = dict(
    small_src=pltpu.VMEM((2, 16, 128), F32),
    small=pltpu.VMEM((NZ, 2, 16, D), F32),
    wqkv=pltpu.VMEM((2, 3, NZ, HD, D), BF),
    wout=pltpu.VMEM((2, NZ, HD, D), BF),
    wfc1=pltpu.VMEM((2, D, 512), BF),
    wfc2=pltpu.VMEM((2, 512, D), BF),
    start=pltpu.VMEM((ROWS, D), BF),
    first_grad=pltpu.VMEM((ROWS, D), BF),
    ending=pltpu.VMEM((ROWS, D), BF),
    back=pltpu.VMEM((ROWS, D), BF),
    stream=pltpu.VMEM((3, ROWS, D), F32),
    mid=pltpu.VMEM((2, ROWS, D), F32),
    branch=pltpu.VMEM((2, 2, ROWS, D), F32),
    grad=pltpu.VMEM((ROWS, D), F32),
    normed=pltpu.VMEM((2, 2, NX, CHUNKS, 2, PART, D), BF),
    q=pltpu.VMEM((2, *HEADS), BF),
    k=pltpu.VMEM((2, *HEADS), BF),
    v=pltpu.VMEM((2, *HEADS), BF),
    mixed=pltpu.VMEM((2, *HEADS), BF),
    lse=pltpu.VMEM((2, NX, 2, 1, 2 * ROWS), F32),
    hidden=pltpu.VMEM((2, NX, 2 * ROWS, 512), BF),
    slope=pltpu.VMEM((2, NX, 2 * ROWS, 512), BF),
    mk=pltpu.VMEM((2, *HEADS), BF),
    mv=pltpu.VMEM((2, *HEADS), BF),
    turned=pltpu.VMEM((NX, 128, 2 * ROWS), BF),
    mixt=pltpu.VMEM((128, 2 * ROWS), F32),
    gath=pltpu.VMEM((2, NX, CHUNKS, 2, PART, D), BF),
    pre=pltpu.VMEM((NX, 2 * ROWS, 512), BF),
    gmix=pltpu.VMEM(HEADS, BF),
    dq=pltpu.VMEM(HEADS, BF),
    dk=pltpu.VMEM((SEQ, 128), F32),
    dv=pltpu.VMEM((SEQ, 128), F32),
    dall=pltpu.VMEM((NX, 2 * ROWS, 384), BF),
    sums=pltpu.VMEM((2, 2, 8, D), F32),
    dqkv=pltpu.VMEM((3, NZ, HD, D), BF),
    dout=pltpu.VMEM((NZ, HD, D), BF),
    dfc1=pltpu.VMEM((D, 512), BF),
    dfc2=pltpu.VMEM((512, D), BF),
    vec_src=pltpu.VMEM((16, D), F32),
    unit_src=pltpu.VMEM((NZ, 8, 128), F32),
    vec_sum=pltpu.VMEM((16, 128), F32),
    land_qkv=pltpu.VMEM((2, NF * NZ, *PIECE["qkv"]), BF),
    land_out=pltpu.VMEM((2, NF * NZ, *PIECE["out"]), BF),
    land_fc1=pltpu.VMEM((2, NF * NZ, *PIECE["fc1"]), BF),
    land_fc2=pltpu.VMEM((2, NF * NZ, *PIECE["fc2"]), BF),
    land_vec=pltpu.VMEM((NF * NZ, *PIECE["vec"]), F32),
    land_unit=pltpu.VMEM((NF * NZ, *PIECE["unit"]), F32),
    land_ring=pltpu.VMEM((2 * NX, *PIECE["vec"]), F32),
    small_sems=sems(NF * NZ),
    qkv_sems=sems(2, NF * NZ),
    out_sems=sems(2, NF * NZ),
    fc1_sems=sems(2, NF * NZ),
    fc2_sems=sems(2, NF * NZ),
    dqkv_sems=sems(2, NF * NZ),
    dout_sems=sems(2, NF * NZ),
    dfc1_sems=sems(2, NF * NZ),
    dfc2_sems=sems(2, NF * NZ),
    vec_sems=sems(NF * NZ),
    unit_sems=sems(NF * NZ),
    swap_sems=sems(4),
    ring_sems=sems(2 * NX),
    ring=RING_SCRATCH,
)


def scratch_list():
    flat = []
    for item in SCRATCH.values():
        flat += item if isinstance(item, list) else [item]
    return flat


class Refs:
    def __init__(self, flat):
        flat = list(flat)
        for name, item in SCRATCH.items():
            if isinstance(item, list):
                setattr(self, name, [flat.pop(0) for _ in item])
            else:
                setattr(self, name, flat.pop(0))


IN = ("tokens", "cotangent", "w_qkv", "qv_bias", "w_out", "w_fc1", "fc1_bias", "w_fc2")
IN += ("norm_gain", "norm_bias", "layer_scale", "out_bias")
OUT = ("out_tokens", "grad_tokens", "g_qkv", "g_out", "g_fc1", "g_fc2", "g_vec", "g_shift", "g_unit")


def pair(send_recv, *at):
    return [s.at[at] for s in send_recv]


class Program:
    def __init__(self, flat):
        for name, ref in zip(IN + OUT, flat):
            setattr(self, name, ref)
        self.r = Refs(flat[len(IN + OUT) :])
        self.ring = Ring(*self.r.ring)

    def small_job(self):
        r = self.r
        return Gather("small", r.small_src, r.small, *r.small_sems)

    def head_jobs(self, l):
        r = self.r
        return (
            Gather("qkv", self.w_qkv.at[l], r.wqkv.at[l], *pair(r.qkv_sems, l)),
            Gather("out", self.w_out.at[l], r.wout.at[l], *pair(r.out_sems, l)),
        )

    def unit_jobs(self, l):
        r = self.r
        return (
            Gather("fc1", self.w_fc1.at[l], r.wfc1.at[l], *pair(r.fc1_sems, l)),
            Gather("fc2", self.w_fc2.at[l], r.wfc2.at[l], *pair(r.fc2_sems, l)),
        )

    def head_sums(self, l):
        r = self.r
        return (
            Scatter("qkv", r.dqkv, r.land_qkv.at[l], *pair(r.dqkv_sems, l)),
            Scatter("out", r.dout, r.land_out.at[l], *pair(r.dout_sems, l)),
        )

    def unit_sums(self, l):
        r = self.r
        return (
            Scatter("fc1", r.dfc1, r.land_fc1.at[l], *pair(r.dfc1_sems, l)),
            Scatter("fc2", r.dfc2, r.land_fc2.at[l], *pair(r.dfc2_sems, l)),
        )

    def finish_heads(self, l):
        qkv, out = self.head_sums(l)
        self.g_qkv[l] = qkv.total()
        self.g_out[l] = out.total()

    def finish_units(self, l):
        fc1, fc2 = self.unit_sums(l)
        self.g_fc1[l] = fc1.total()
        self.g_fc2[l] = fc2.total()

    def swap(self, i, src, dst):
        return Swap(src, dst, *pair(self.r.swap_sems, i))

    def run(self):
        r = self.r
        greeted = greet()
        for l in range(2):
            at = 0
            for ref in (self.norm_gain, self.norm_bias, self.layer_scale, self.out_bias):
                r.small_src[l, at : at + 2, :] = ref[l].astype(F32)
                at += 2
            bias = self.fc1_bias[...].astype(F32)[l : l + 1]
            r.small_src[l, 8:9, :] = bias[:, :128]
            r.small_src[l, 9:10, :] = bias[:, 128:]
            r.small_src[l, 10:11, :] = self.qv_bias[...].astype(F32)[l : l + 1]
            r.small_src[l, 11:16, :] = jnp.zeros((5, 128), F32)
        greeted()
        tokens = self.swap(0, self.tokens, r.start)
        self.small_job().start()
        tokens.start()
        for job in self.head_jobs(0):
            job.start()
        tokens.wait()
        r.stream[0] = r.start[...].astype(F32)
        self.small_job().wait()
        lax.fori_loop(0, 2, self.forward, 0)
        r.ending[...] = r.stream[2].astype(BF)
        self.cotangent_swap().wait()
        r.grad[...] = r.first_grad[...].astype(F32)
        lax.fori_loop(0, 2, self.backward, 0)
        r.start[...] = r.grad[...].astype(BF)
        back = self.swap(3, r.start, r.back)
        back.start()
        self.last_sums()
        self.ending_swap().wait()
        back.wait()
        self.grad_tokens[...] = r.back[...].astype(F32)

    def cotangent_swap(self):
        return self.swap(1, self.cotangent, self.r.first_grad)

    def ending_swap(self):
        return self.swap(2, self.r.ending, self.out_tokens)

    def forward(self, l, _):
        self.attn_forward(l)
        self.mlp_forward(l)
        return 0

    def backward(self, i, _):
        self.mlp_backward(1 - i)
        self.attn_backward(1 - i)
        return 0

    def attn_forward(self, l):
        r, ring = self.r, self.ring
        vec = r.small[0, l]
        normal, _ = norm_parts(r.stream[l])
        ring.set_own(r.normed.at[l, 0], (normal * vec[0:1] + vec[2:3]).astype(BF))
        bias_a, bias_b = r.small[0, l][10:11, 0:128], r.small[1, l][10:11, 0:128]
        shift = jnp.concatenate(
            [
                bias_a[:, :HD],
                bias_b[:, :HD],
                jnp.zeros((1, 128), F32),
                bias_a[:, HD:],
                bias_b[:, HD:],
            ],
            axis=1,
        )
        for job in self.head_jobs(l):
            job.wait()
        for job in self.unit_jobs(l):
            job.start()
        weights = r.wqkv[l].reshape(3 * 2 * HD, D)

        def project(who):
            at = ring.at[who]
            qkv = (dot_nt(ring.rows(who), weights) + shift).astype(BF)
            keys, values = qkv[:, 128:256], qkv[:, 256:]
            r.q[l, at] = qkv[:, :128] * 0.125
            r.k[l, at] = keys
            r.v[l, at] = values
            head = lane_head((2 * ROWS, 128))
            for h in range(2):
                r.mk[h, at] = jnp.where(head == h, keys, jnp.zeros_like(keys))
            r.turned[at] = values.astype(F32).T.astype(BF)

        ring.by_blocks(project)
        pl.when(l == 0)(self.cotangent_swap().start)

        def attend(who):
            at = ring.at[who]

            def head_step(h, _):
                scores = dot_nt(r.mk[h].reshape(SEQ, 128), r.q[l, at])
                highest = jnp.max(scores, axis=0, keepdims=True)
                weights = jnp.exp(scores - highest)
                total = jnp.sum(weights, axis=0, keepdims=True)
                probs = (weights * (1.0 / total)).astype(BF)
                span = pl.ds(pl.multiple_of(h * HD, HD), HD)
                mixed = jnp.zeros((HD, 2 * ROWS), F32)
                for part in range(NX):
                    mixed = mixed + dot_nn(
                        r.turned[part, span, :],
                        probs[part * 2 * ROWS : (part + 1) * 2 * ROWS],
                    )
                r.mixt[span, :] = mixed
                r.lse[l, at, h] = highest + jnp.log(total)
                return 0

            lax.fori_loop(0, 2, head_step, 0)
            mixed = r.mixt[...].T.astype(BF)
            r.mixed[l, at] = mixed
            return dot_nn(mixed, r.wout[l].reshape(2 * HD, D))

        ring.back_by_blocks(attend)
        ring.merge(0)
        ring.merge(1)
        branch = ring.finish() + vec[6:7]
        r.branch[l, 0] = branch
        r.mid[l] = r.stream[l] + vec[4:5] * branch
        ring.drain()

    def mlp_forward(self, l):
        r, ring = self.r, self.ring
        vec = r.small[0, l]
        normal, _ = norm_parts(r.mid[l])
        ring.set_own(r.normed.at[l, 1], (normal * vec[1:2] + vec[3:4]).astype(BF))
        bias = jnp.concatenate(
            [r.small[z, l][row : row + 1, 0:128] for z in range(NZ) for row in (8, 9)], axis=1
        )
        for job in self.unit_jobs(l):
            job.wait()

        @pl.when(l == 0)
        def _():
            for job in self.head_jobs(1):
                job.start()

        def step(ch, who):
            at = ring.at[who]
            span = slice(ch * 2 * PART, (ch + 1) * 2 * PART)
            pre = dot_nn(ring.chunk(ch, who), r.wfc1[l]) + bias
            phi = 0.5 * (1.0 + lax.erf(pre * ROOT_HALF))
            hidden = (pre * phi).astype(BF)
            slope = phi + pre * INV_ROOT_TAU * jnp.exp(-0.5 * pre * pre)
            r.slope[l, at, span, :] = slope.astype(BF)
            r.hidden[l, at, span, :] = hidden
            ring.put(ch, who, dot_nn(hidden, r.wfc2[l]))

        ring.by_chunks(step)
        ring.merge(1)
        branch = ring.finish() + vec[7:8]
        r.branch[l, 1] = branch
        r.stream[l + 1] = r.mid[l] + vec[5:6] * branch
        ring.drain()

    def begin_backward(self, l, i, gath):
        r = self.r
        g = r.grad[...]
        scaled = r.small[0, l][4 + i : 5 + i] * g
        self.ring.set_own(gath, scaled.astype(BF))
        r.sums[l, i] = jnp.zeros((8, D), F32)
        r.sums[l, i, 2:3, :] = row_sum(r.branch[l, i] * g)
        r.sums[l, i, 3:4, :] = row_sum(scaled)

    def end_backward(self, l, i, stream):
        r = self.r
        back = self.ring.finish()
        normal, inverse = norm_parts(stream)
        r.sums[l, i, 0:1, :] = row_sum(back * normal)
        r.sums[l, i, 1:2, :] = row_sum(back)
        gain = r.small[0, l][i : i + 1]
        r.grad[...] += norm_backward(back, normal, inverse, gain)
        self.ring.drain()

    def mlp_backward(self, l):
        r, ring = self.r, self.ring
        gath = r.gath.at[0]
        self.begin_backward(l, 1, gath)

        def step(ch, who):
            at = ring.at[who]
            span = slice(ch * 2 * PART, (ch + 1) * 2 * PART)
            back = dot_nt(ring.chunk(ch, who), r.wfc2[l]) * r.slope[l, at, span, :].astype(F32)
            back = back.astype(BF)
            r.pre[at, span, :] = back
            ring.put(ch, who, dot_nt(back, r.wfc1[l]))

        ring.by_chunks(step)
        fc1, fc2 = self.unit_sums(l)
        r.dfc2[...] = dot_tn(
            r.hidden[l].reshape(SEQ, 512), gath[...].reshape(SEQ, D)
        ).astype(BF)
        fc2.start()
        ring.merge(1)
        r.dfc1[...] = dot_tn(
            r.normed[l, 1].reshape(SEQ, D), r.pre[...].reshape(SEQ, 512)
        ).astype(BF)
        fc1.start()
        r.sums[l, 1, 4:5, 0:512] = row_sum(r.pre[...].reshape(SEQ, 512).astype(F32))

        @pl.when(l == 0)
        def _():
            self.finish_heads(1)

        self.end_backward(l, 1, r.mid[l])

    def attn_backward(self, l):
        r, ring = self.r, self.ring
        gath = r.gath.at[1]
        self.begin_backward(l, 0, gath)
        head = lane_head((2 * ROWS, 128))
        for part in range(NX):
            keys, values = r.k[l, part], r.v[l, part]
            for h in range(2):
                r.mk[h, part] = jnp.where(head == h, keys, jnp.zeros_like(keys))
                r.mv[h, part] = jnp.where(head == h, values, jnp.zeros_like(values))
            r.turned[part] = keys.astype(F32).T.astype(BF)
        r.dk[...] = jnp.zeros((SEQ, 128), F32)
        r.dv[...] = jnp.zeros((SEQ, 128), F32)

        def attend(who):
            at = ring.at[who]
            if who == FAR:
                pl.when(l == 1)(self.ending_swap().start)
            r.gmix[at] = dot_nt(ring.rows(who), r.wout[l].reshape(2 * HD, D)).astype(BF)

            def head_step(h, _):
                queries, mine = r.q[l, at], r.gmix[at]
                probs = jnp.exp(dot_nt(r.mk[h].reshape(SEQ, 128), queries) - r.lse[l, at, h])
                back = dot_nt(r.mv[h].reshape(SEQ, 128), mine)
                delta = jnp.sum(probs * back, axis=0, keepdims=True)
                dscores = (probs * (back - delta)).astype(BF)
                span = pl.ds(pl.multiple_of(h * HD, HD), HD)
                turned = jnp.zeros((HD, 2 * ROWS), F32)
                for part in range(NX):
                    turned = turned + dot_nn(
                        r.turned[part, span, :],
                        dscores[part * 2 * ROWS : (part + 1) * 2 * ROWS],
                    )
                r.mixt[span, :] = turned * 0.125
                mask = head == h
                r.dk[...] += dot_nn(dscores, jnp.where(mask, queries, jnp.zeros_like(queries)))
                r.dv[...] += dot_nn(
                    probs.astype(BF), jnp.where(mask, mine, jnp.zeros_like(mine))
                )
                return 0

            lax.fori_loop(0, 2, head_step, 0)
            r.dq[at] = r.mixt[...].T.astype(BF)

        ring.by_blocks(attend)
        for part in range(NX):
            span = slice(part * 2 * ROWS, (part + 1) * 2 * ROWS)
            r.dall[part] = jnp.concatenate(
                [r.dq[part], r.dk[span, :].astype(BF), r.dv[span, :].astype(BF)], axis=1
            )
        weights = r.wqkv[l].reshape(3 * 2 * HD, D)
        ring.back_by_blocks(lambda who: dot_nn(r.dall[ring.at[who]], weights))
        qkv, out = self.head_sums(l)
        whole = r.dall[...].reshape(SEQ, 384)
        dqkv = dot_tn(whole, r.normed[l, 0].reshape(SEQ, D)).astype(BF)
        r.dqkv[...] = dqkv.reshape(3, NZ, HD, D)
        qkv.start()
        ring.merge(0)
        ring.merge(1)
        dout = dot_tn(r.mixed[l].reshape(SEQ, 128), gath[...].reshape(SEQ, D)).astype(BF)
        r.dout[...] = dout.reshape(NZ, HD, D)
        out.start()
        unit = row_sum(whole.astype(F32))
        r.sums[l, 0, 4:5, 0:256] = jnp.concatenate(
            [
                unit[:, 0:HD],
                unit[:, 256 : 256 + HD],
                unit[:, HD:128],
                unit[:, 256 + HD : 384],
            ],
            axis=1,
        )
        self.finish_units(l)
        self.end_backward(l, 0, r.stream[l])

    def last_sums(self):
        r = self.r
        for l in range(2):
            for i in range(2):
                sums = r.sums[l, i]
                for kind in range(4):
                    row = kind * 4 + l * 2 + i
                    r.vec_src[row : row + 1, :] = sums[kind : kind + 1]
            heads, units = r.sums[l, 0], r.sums[l, 1]
            for z in range(NZ):
                for at, row in ((0, l * 2), (128, l * 2 + 1)):
                    at = at + z * 256
                    r.unit_src[z, row : row + 1, :] = units[4:5, at : at + 128]
                r.unit_src[z, 4 + l : 5 + l, :] = heads[4:5, z * 128 : (z + 1) * 128]
                r.unit_src[z, 6 + l : 7 + l, :] = jnp.zeros((1, 128), F32)
        vec = Scatter("vec", r.vec_src, r.land_vec, *r.vec_sems)
        unit = Scatter("unit", r.unit_src, r.land_unit, *r.unit_sems)
        vec.start()
        unit.start()
        r.vec_sum[...] = vec.total()

        def copy(step):
            return pltpu.make_async_remote_copy(
                src_ref=r.vec_sum,
                dst_ref=r.land_ring.at[step],
                send_sem=r.ring_sems[0].at[step],
                recv_sem=r.ring_sems[1].at[step],
                device_id=ring_id(step),
                device_id_type=MESH,
            )

        for s in range(1, 2 * NX):
            copy(s).start()
        units = unit.total()
        self.g_shift[...] = units[4:6]
        for l in range(2):
            self.g_unit[l : l + 1, 0:128] = units[2 * l : 2 * l + 1]
            self.g_unit[l : l + 1, 128:256] = units[2 * l + 1 : 2 * l + 2]
        self.finish_heads(0)
        total = r.vec_sum[...]
        for s in range(1, 2 * NX):
            copy(s).wait()
            total = total + r.land_ring[s]
        self.g_vec[...] = total


def whole_kernel(*flat):
    Program(flat).run()


def run_whole(*args):
    outs = [
        jax.ShapeDtypeStruct((ROWS, D), BF),
        jax.ShapeDtypeStruct((ROWS, D), F32),
        jax.ShapeDtypeStruct((2, 3, HD, 128), F32),
        jax.ShapeDtypeStruct((2, HD, 128), F32),
        jax.ShapeDtypeStruct((2, 128, 256), F32),
        jax.ShapeDtypeStruct((2, 256, 128), F32),
        jax.ShapeDtypeStruct((16, 128), F32),
        jax.ShapeDtypeStruct((2, 128), F32),
        jax.ShapeDtypeStruct((2, 256), F32),
    ]
    whole = pl.BlockSpec(memory_space=pltpu.VMEM)
    return pl.pallas_call(
        whole_kernel,
        out_shape=outs,
        in_specs=[whole] * len(args),
        out_specs=[whole] * len(outs),
        scratch_shapes=scratch_list(),
        compiler_params=pltpu.CompilerParams(
            collective_id=0, has_side_effects=True, vmem_limit_bytes=VMEM_BYTES
        ),
        cost_estimate=pl.CostEstimate(
            flops=24_000_000_000, bytes_accessed=8_000_000, transcendentals=10_000_000
        ),
    )(*args)


def on_device(
    tokens,
    cotangent,
    w_qkv,
    qv_bias,
    w_out,
    w_fc1,
    fc1_bias,
    w_fc2,
    norm_gain,
    norm_bias,
    layer_scale,
    out_bias,
):
    out_tokens, grad_tokens, g_qkv, g_out, g_fc1, g_fc2, g_vec, g_shift, g_unit = run_whole(
        tokens,
        cotangent,
        jnp.swapaxes(w_qkv[:, :, 0, :], 1, 2).reshape(2, 3, HD, 128),
        qv_bias.reshape(2, 128),
        w_out.reshape(2, HD, 128),
        w_fc1,
        fc1_bias,
        w_fc2,
        norm_gain,
        norm_bias,
        layer_scale,
        out_bias,
    )
    vec = g_vec.reshape(4, 2, 2, 128)
    return (
        out_tokens,
        grad_tokens,
        jnp.swapaxes(g_qkv.reshape(2, 3 * HD, 128), 1, 2)[:, :, None, :],
        g_shift[:, None, :],
        g_out[:, None],
        g_fc1,
        g_unit,
        g_fc2,
        vec[0],
        vec[1],
        vec[2],
        vec[3],
    )


def solution(mesh):
    split = Mesh(
        mesh.devices.reshape(mesh.shape["fsdp"], NX, NZ, 2),
        ("fsdp", "tensor_0", "tensor_1", "tensor_2"),
    )
    return jax.shard_map(
        on_device,
        mesh=split,
        in_specs=(
            P(FSDP_TENSOR, None),
            P(FSDP_TENSOR, None),
            P(None, "fsdp", TENSOR, None),
            P(None, TENSOR, None),
            P(None, TENSOR, None, "fsdp"),
            P(None, "fsdp", TENSOR),
            P(None, TENSOR),
            P(None, TENSOR, "fsdp"),
            P(None, None, "fsdp"),
            P(None, None, "fsdp"),
            P(None, None, "fsdp"),
            P(None, None, "fsdp"),
        ),
        out_specs=(
            P(FSDP_TENSOR, None),
            P(FSDP_TENSOR, None),
            P(None, "fsdp", TENSOR, None),
            P(None, TENSOR, None),
            P(None, TENSOR, None, "fsdp"),
            P(None, "fsdp", TENSOR),
            P(None, TENSOR),
            P(None, TENSOR, "fsdp"),
            P(None, None, "fsdp"),
            P(None, None, "fsdp"),
            P(None, None, "fsdp"),
            P(None, None, "fsdp"),
        ),
        check_vma=False,
    )
```

```python
import jax
import jax.numpy as jnp
from jax import lax
from jax.experimental import pallas as pl
from jax.experimental.pallas import tpu as pltpu
from jax.sharding import Mesh
from jax.sharding import PartitionSpec as P

D = 1024
HD = 64
SEQ = 1024
ROWS = 128
NX = 4
NF = 8
NZ = 2
F32 = jnp.float32
BF = jnp.bfloat16
TENSOR = ("tensor_0", "tensor_1", "tensor_2")
FSDP_TENSOR = ("fsdp", "tensor_0", "tensor_1", "tensor_2")
MESH = pl.DeviceIdType.MESH
EPS = 1e-06
ROOT_HALF = 0.7071067811865476
INV_ROOT_TAU = 0.3989422804014327
CHUNKS = 2
PART = ROWS // CHUNKS
HALF = PART // 2
GCOPIES = 10
SCOPIES = 10
TOP = pl.ds(0, HALF)
BOTTOM = pl.ds(HALF, HALF)
VMEM_BYTES = 62 * 1024 * 1024
OWN, LEFT, RIGHT, FAR = 0, 1, 2, 3


def dot_nn(left, right):
    return lax.dot_general(left, right, (((1,), (0,)), ((), ())), preferred_element_type=F32)


def dot_nt(left, right):
    return lax.dot_general(left, right, (((1,), (1,)), ((), ())), preferred_element_type=F32)


def dot_tn(left, right):
    return lax.dot_general(left, right, (((0,), (0,)), ((), ())), preferred_element_type=F32)


def norm_parts(stream):
    centre = stream - jnp.mean(stream, axis=-1, keepdims=True)
    inverse = lax.rsqrt(jnp.mean(centre * centre, axis=-1, keepdims=True) + EPS)
    return centre * inverse, inverse


def norm_backward(grad_out, normal, inverse, gain):
    scaled = grad_out * gain
    return inverse * (
        scaled
        - jnp.mean(scaled, axis=-1, keepdims=True)
        - normal * jnp.mean(scaled * normal, axis=-1, keepdims=True)
    )


def group_index():
    return lax.axis_index("fsdp"), lax.axis_index("tensor_1")


def group_peer(step):
    f, z = group_index()
    at = lax.rem(f * NZ + z + step, NF * NZ)
    return at // NZ, lax.rem(at, NZ)


def group_id(step):
    f, z = group_peer(step)
    return {"fsdp": f, "tensor_1": z}


def cols(f, width=128):
    return pl.ds(pl.multiple_of(f * width, width), width)


VIEWS = {
    "qkv": lambda ref, f, z: ref.at[:, z, :, cols(f)],
    "out": lambda ref, f, z: ref.at[z, :, cols(f)],
    "small": lambda ref, f, z: ref.at[z, :, :, cols(f)],
    "fc1": lambda ref, f, z: ref.at[cols(f), cols(z, 256)],
    "fc2": lambda ref, f, z: ref.at[cols(z, 256), cols(f)],
    "vec": lambda ref, f, z: ref.at[:, cols(f)],
    "unit": lambda ref, f, z: ref.at[z],
}


def each_peer(act):
    def step(s, _):
        act(s)
        return 0

    lax.fori_loop(1, NF * NZ, step, 0)


class Gather:
    def __init__(self, kind, src, dst, send, recv):
        self.view, self.src, self.dst = VIEWS[kind], src, dst
        self.send, self.recv = send, recv

    def copy(self, step):
        return pltpu.make_async_remote_copy(
            src_ref=self.src,
            dst_ref=self.view(self.dst, *group_index()),
            send_sem=self.send.at[step],
            recv_sem=self.recv.at[step],
            device_id=group_id(step),
            device_id_type=MESH,
        )

    def local(self):
        return pltpu.make_async_copy(
            self.src, self.view(self.dst, *group_index()), self.send.at[0]
        )

    def start(self):
        self.local().start()
        each_peer(lambda s: self.copy(s).start())

    def wait(self):
        self.local().wait()
        each_peer(lambda s: self.copy(s).wait())


class Relay:
    def __init__(self, kind, src, dst, send, recv, y_first):
        self.view, self.src, self.dst = VIEWS[kind], src, dst
        self.send, self.recv, self.y_first = send, recv, y_first
        f, z = group_index()
        self.y, self.z = f // 2, z * 2 + lax.rem(f, 2)

    def place(self, first, second):
        y, z = (first, second) if self.y_first else (second, first)
        y, z = lax.rem(self.y + y, 4), lax.rem(self.z + z, 4)
        return y * 2 + lax.rem(z, 2), z // 2

    def copy(self, first, second):
        if second:
            f, z = self.place(0, second)
            origin = self.place(4 - first if first else 0, 0)
        else:
            f, z = self.place(first, 0)
            origin = self.place(0, 0)
        there = self.view(self.dst, *origin)
        return pltpu.make_async_remote_copy(
            src_ref=there if first and second else self.src,
            dst_ref=there,
            send_sem=self.send.at[first * 4 + second],
            recv_sem=self.recv.at[first * 4 + second],
            device_id={"fsdp": f, "tensor_1": z},
            device_id_type=MESH,
        )

    def local(self):
        return pltpu.make_async_copy(
            self.src, self.view(self.dst, *self.place(0, 0)), self.send.at[0]
        )

    def start(self):
        self.local().start()
        for step in (2, 1, 3):
            self.copy(step, 0).start()
        for step in (2, 1, 3):
            self.copy(0, step).start()

    def pump(self):
        for first in (1, 3, 2):
            self.copy(first, 0).wait_recv()
            for second in (2, 1, 3):
                self.copy(first, second).start()

    def wait(self):
        self.local().wait()
        for first in range(1, 4):
            self.copy(first, 0).wait_send()
        for first in range(4):
            for second in range(1, 4):
                self.copy(first, second).wait()


class Scatter:
    def __init__(self, kind, src, land, send, recv):
        self.view, self.src, self.land = VIEWS[kind], src, land
        self.send, self.recv = send, recv

    def copy(self, step):
        return pltpu.make_async_remote_copy(
            src_ref=self.view(self.src, *group_peer(step)),
            dst_ref=self.land.at[step],
            send_sem=self.send.at[step],
            recv_sem=self.recv.at[step],
            device_id=group_id(step),
            device_id_type=MESH,
        )

    def local(self):
        return pltpu.make_async_copy(
            self.view(self.src, *group_index()), self.land.at[0], self.send.at[0]
        )

    def start(self):
        self.local().start()
        each_peer(lambda s: self.copy(s).start())

    def total(self):
        self.local().wait()
        each_peer(lambda s: self.copy(s).wait())
        return sum(self.land[s].astype(F32) for s in range(NF * NZ))


class Swap:
    def __init__(self, src, dst, send, recv):
        x, z = lax.axis_index("tensor_0"), lax.axis_index("tensor_1")
        self.moves = lax.rem(x // 2 + z, 2) == 1
        self.remote = pltpu.make_async_remote_copy(
            src_ref=src,
            dst_ref=dst,
            send_sem=send,
            recv_sem=recv,
            device_id=swap_id(),
            device_id_type=MESH,
        )
        self.stay = pltpu.make_async_copy(src, dst, send)

    def start(self):
        pl.when(self.moves)(self.remote.start)
        pl.when(jnp.logical_not(self.moves))(self.stay.start)

    def wait(self):
        pl.when(self.moves)(self.remote.wait)
        pl.when(jnp.logical_not(self.moves))(self.stay.wait)


def swap_id():
    x, z = lax.axis_index("tensor_0"), lax.axis_index("tensor_1")
    return {"tensor_0": lax.rem(x + 2, NX), "tensor_1": 1 - z}


def ring_id(step):
    x, c = lax.axis_index("tensor_0"), lax.axis_index("tensor_2")
    at = lax.rem(x * 2 + c + step, 2 * NX)
    return {"tensor_0": at // 2, "tensor_2": lax.rem(at, 2)}


def greet():
    barrier = pltpu.get_barrier_semaphore()

    def signal(where):
        pl.semaphore_signal(barrier, inc=1, device_id=where, device_id_type=MESH)

    for s in range(1, 2 * NX):
        signal(ring_id(s))
    signal(swap_id())
    each_peer(lambda s: signal(group_id(s)))
    return lambda: pl.semaphore_wait(barrier, 2 * NX + NF * NZ - 1)


class Ring:
    def __init__(self, part, pin, sout, rin, held, gsend, grecv, ssend, srecv):
        self.x, self.c = lax.axis_index("tensor_0"), lax.axis_index("tensor_2")
        self.at = [self.x] + [lax.rem(self.x + s, NX) for s in (3, 1, 2)]
        self.part, self.pin = part, pin
        self.sout, self.rin, self.held = sout, rin, held
        self.gsend, self.grecv, self.ssend, self.srecv = gsend, grecv, ssend, srecv
        self.left = {"tensor_0": self.at[LEFT]}
        self.right = {"tensor_0": self.at[RIGHT]}
        self.twin = {"tensor_2": 1 - self.c}

    def gcopy(self, ch, i):
        who, rows, to = (
            (OWN, None, self.twin),
            (OWN, TOP, self.right),
            (OWN, BOTTOM, self.right),
            (OWN, BOTTOM, self.left),
            (OWN, TOP, self.left),
            (LEFT, TOP, self.right),
            (RIGHT, BOTTOM, self.left),
            (LEFT, None, self.twin),
            (RIGHT, None, self.twin),
            (FAR, None, self.twin),
        )[i]
        ref = self.gath.at[self.at[who], ch, self.c]
        if rows is not None:
            ref = ref.at[rows]
        return pltpu.make_async_remote_copy(
            src_ref=ref,
            dst_ref=ref,
            send_sem=self.gsend.at[ch * GCOPIES + i],
            recv_sem=self.grecv.at[ch * GCOPIES + i],
            device_id=to,
            device_id_type=MESH,
        )

    def got(self, ch, i):
        self.gcopy(ch, i).wait_recv()

    def go(self, ch, *which):
        for i in which:
            self.gcopy(ch, i).start()

    def set_own(self, gath, rows):
        self.gath = gath
        for ch in range(CHUNKS):
            gath[self.x, ch, self.c] = rows[ch * PART : (ch + 1) * PART]
        for ch in range(CHUNKS):
            self.go(ch, 1, 3, 2, 4, 0)

    def near(self, ch):
        self.got(ch, 1)
        self.go(ch, 5)
        self.got(ch, 3)
        self.go(ch, 6)
        self.got(ch, 2)
        self.go(ch, 7)
        self.got(ch, 4)
        self.go(ch, 8)

    def far(self, ch):
        self.got(ch, 5)
        self.got(ch, 6)
        self.go(ch, 9)

    def arrive(self, ch, who):
        self.got(ch, (0, 7, 8, 9)[who])

    def arrive_both(self, who):
        self.arrive(0, who)
        self.arrive(1, who)

    def chunk(self, ch, who):
        return self.gath[self.at[who], ch].reshape(2 * PART, D)

    def rows(self, who):
        return self.gath[self.at[who]].reshape(2 * ROWS, D)

    def pcopy(self, ch, who):
        return pltpu.make_async_remote_copy(
            src_ref=self.part.at[ch, who, 1 - self.c],
            dst_ref=self.pin.at[ch, who],
            send_sem=self.ssend.at[ch * SCOPIES + 6 + who],
            recv_sem=self.srecv.at[ch * SCOPIES + 6 + who],
            device_id=self.twin,
            device_id_type=MESH,
        )

    def scopy(self, ch, i):
        return pltpu.make_async_remote_copy(
            src_ref=self.sout.at[ch, i],
            dst_ref=self.rin.at[ch, i],
            send_sem=self.ssend.at[ch * SCOPIES + i],
            recv_sem=self.srecv.at[ch * SCOPIES + i],
            device_id=self.left if i in (1, 4, 5) else self.right,
            device_id_type=MESH,
        )

    def put(self, ch, who, value):
        self.part[ch, who] = value.astype(BF).reshape(2, PART, D)
        self.pcopy(ch, who).start()

    def put_both(self, who, value):
        self.put(0, who, value[: 2 * PART])
        self.put(1, who, value[2 * PART :])

    def send(self, ch, i, value):
        self.sout[ch, i] = value.astype(BF)
        self.scopy(ch, i).start()

    def both_cores(self, ch, who):
        self.pcopy(ch, who).wait_recv()
        return self.part[ch, who, self.c].astype(F32) + self.pin[ch, who].astype(F32)

    def flush(self, ch, who):
        total = self.both_cores(ch, who)
        if who == FAR:
            self.send(ch, 0, total[:HALF])
            self.send(ch, 1, total[HALF:])
        elif who == RIGHT:
            self.send(ch, 2, total[HALF:])
            self.held[ch, 0] = total[:HALF]
        else:
            self.send(ch, 4, total[:HALF])
            self.held[ch, 1] = total[HALF:]

    def flush_both(self, *which):
        for who in which:
            for ch in range(CHUNKS):
                self.flush(ch, who)

    def merge(self, ch):
        self.scopy(ch, 0).wait_recv()
        self.send(ch, 3, self.held[ch, 0] + self.rin[ch, 0].astype(F32))
        self.scopy(ch, 1).wait_recv()
        self.send(ch, 5, self.held[ch, 1] + self.rin[ch, 1].astype(F32))

    def finish(self):
        rows = []
        for ch in range(CHUNKS):
            total = self.both_cores(ch, OWN)
            for i in (2, 4, 3, 5):
                self.scopy(ch, i).wait_recv()
            rin = [self.rin[ch, i].astype(F32) for i in (2, 3, 4, 5)]
            rows += [total[:HALF] + rin[1] + rin[2], total[HALF:] + rin[0] + rin[3]]
        return jnp.concatenate(rows, axis=0)

    def drain(self):
        for ch in range(CHUNKS):
            for i in range(GCOPIES):
                self.gcopy(ch, i).wait_send()
            for i in range(6):
                self.scopy(ch, i).wait_send()
            for i in range(4):
                self.pcopy(ch, i).wait_send()

    def by_chunks(self, step):
        self.arrive(0, OWN)
        step(0, OWN)
        self.near(0)
        self.arrive(1, OWN)
        step(1, OWN)
        for who in (LEFT, RIGHT):
            self.arrive(0, who)
            step(0, who)
        self.near(1)
        self.flush(0, LEFT)
        self.flush(0, RIGHT)
        self.far(0)
        self.arrive(1, LEFT)
        step(1, LEFT)
        self.arrive(0, FAR)
        step(0, FAR)
        self.far(1)
        self.arrive(1, RIGHT)
        step(1, RIGHT)
        self.flush(0, FAR)
        self.arrive(1, FAR)
        step(1, FAR)
        self.flush(1, LEFT)
        self.flush(1, RIGHT)
        self.flush(1, FAR)
        self.merge(0)

    def by_blocks(self, step):
        self.arrive_both(OWN)
        step(OWN)
        self.near(0)
        self.near(1)
        self.arrive_both(LEFT)
        step(LEFT)
        self.far(0)
        self.far(1)
        self.arrive_both(RIGHT)
        step(RIGHT)
        self.arrive_both(FAR)
        step(FAR)

    def back_by_blocks(self, value):
        for who in (FAR, LEFT, RIGHT, OWN):
            self.put_both(who, value(who))
            if who == LEFT:
                self.flush_both(FAR)
            elif who == RIGHT:
                self.flush_both(LEFT, RIGHT)


RING_SCRATCH = [
    pltpu.VMEM((CHUNKS, NX, 2, PART, D), BF),
    pltpu.VMEM((CHUNKS, NX, PART, D), BF),
    pltpu.VMEM((CHUNKS, 6, HALF, D), BF),
    pltpu.VMEM((CHUNKS, 6, HALF, D), BF),
    pltpu.VMEM((CHUNKS, 2, HALF, D), F32),
    pltpu.SemaphoreType.DMA((CHUNKS * GCOPIES,)),
    pltpu.SemaphoreType.DMA((CHUNKS * GCOPIES,)),
    pltpu.SemaphoreType.DMA((CHUNKS * SCOPIES,)),
    pltpu.SemaphoreType.DMA((CHUNKS * SCOPIES,)),
]


def lane_head(shape):
    return lax.broadcasted_iota(jnp.int32, shape, len(shape) - 1) // HD


def row_sum(value):
    return jnp.sum(value, axis=0, keepdims=True)


PIECE = {
    "qkv": (3, HD, 128),
    "out": (HD, 128),
    "fc1": (128, 256),
    "fc2": (256, 128),
    "vec": (16, 128),
    "unit": (8, 128),
}
HEADS = (NX, 2 * ROWS, 128)


def sems(*shape):
    return [pltpu.SemaphoreType.DMA(shape)] * 2


SCRATCH = dict(
    small_src=pltpu.VMEM((2, 16, 128), F32),
    small=pltpu.VMEM((NZ, 2, 16, D), F32),
    wqkv=pltpu.VMEM((2, 3, NZ, HD, D), BF),
    wout=pltpu.VMEM((2, NZ, HD, D), BF),
    wfc1=pltpu.VMEM((2, D, 512), BF),
    wfc2=pltpu.VMEM((2, 512, D), BF),
    start=pltpu.VMEM((ROWS, D), BF),
    first_grad=pltpu.VMEM((ROWS, D), BF),
    ending=pltpu.VMEM((ROWS, D), BF),
    back=pltpu.VMEM((ROWS, D), BF),
    stream=pltpu.VMEM((3, ROWS, D), F32),
    mid=pltpu.VMEM((2, ROWS, D), F32),
    branch=pltpu.VMEM((2, 2, ROWS, D), F32),
    grad=pltpu.VMEM((ROWS, D), F32),
    normed=pltpu.VMEM((2, 2, NX, CHUNKS, 2, PART, D), BF),
    q=pltpu.VMEM((2, *HEADS), BF),
    k=pltpu.VMEM((2, *HEADS), BF),
    v=pltpu.VMEM((2, *HEADS), BF),
    mixed=pltpu.VMEM((2, *HEADS), BF),
    lse=pltpu.VMEM((2, NX, 2, 1, 2 * ROWS), F32),
    hidden=pltpu.VMEM((2, NX, 2 * ROWS, 512), BF),
    slope=pltpu.VMEM((2, NX, 2 * ROWS, 512), BF),
    mk=pltpu.VMEM((2, *HEADS), BF),
    mv=pltpu.VMEM((2, *HEADS), BF),
    turned=pltpu.VMEM((NX, 128, 2 * ROWS), BF),
    mixt=pltpu.VMEM((128, 2 * ROWS), F32),
    gath=pltpu.VMEM((2, NX, CHUNKS, 2, PART, D), BF),
    pre=pltpu.VMEM((NX, 2 * ROWS, 512), BF),
    gmix=pltpu.VMEM(HEADS, BF),
    dq=pltpu.VMEM(HEADS, BF),
    dk=pltpu.VMEM((SEQ, 128), F32),
    dv=pltpu.VMEM((SEQ, 128), F32),
    dall=pltpu.VMEM((NX, 2 * ROWS, 384), BF),
    sums=pltpu.VMEM((2, 2, 8, D), F32),
    dqkv=pltpu.VMEM((2, 3, NZ, HD, D), BF),
    dout=pltpu.VMEM((2, NZ, HD, D), BF),
    dfc1=pltpu.VMEM((2, D, 512), BF),
    dfc2=pltpu.VMEM((2, 512, D), BF),
    vec_src=pltpu.VMEM((16, D), F32),
    unit_src=pltpu.VMEM((NZ, 8, 128), F32),
    vec_sum=pltpu.VMEM((16, 128), F32),
    land_qkv=pltpu.VMEM((2, NF * NZ, *PIECE["qkv"]), BF),
    land_out=pltpu.VMEM((2, NF * NZ, *PIECE["out"]), BF),
    land_fc1=pltpu.VMEM((2, NF * NZ, *PIECE["fc1"]), BF),
    land_fc2=pltpu.VMEM((2, NF * NZ, *PIECE["fc2"]), BF),
    land_vec=pltpu.VMEM((NF * NZ, *PIECE["vec"]), F32),
    land_unit=pltpu.VMEM((NF * NZ, *PIECE["unit"]), F32),
    land_ring=pltpu.VMEM((2 * NX, *PIECE["vec"]), F32),
    small_sems=sems(NF * NZ),
    qkv_sems=sems(2, NF * NZ),
    out_sems=sems(2, NF * NZ),
    fc1_sems=sems(2, NF * NZ),
    fc2_sems=sems(2, NF * NZ),
    dqkv_sems=sems(2, NF * NZ),
    dout_sems=sems(2, NF * NZ),
    dfc1_sems=sems(2, NF * NZ),
    dfc2_sems=sems(2, NF * NZ),
    vec_sems=sems(NF * NZ),
    unit_sems=sems(NF * NZ),
    swap_sems=sems(4),
    ring_sems=sems(2 * NX),
    ring=RING_SCRATCH,
)


def scratch_list():
    flat = []
    for item in SCRATCH.values():
        flat += item if isinstance(item, list) else [item]
    return flat


class Refs:
    def __init__(self, flat):
        flat = list(flat)
        for name, item in SCRATCH.items():
            if isinstance(item, list):
                setattr(self, name, [flat.pop(0) for _ in item])
            else:
                setattr(self, name, flat.pop(0))


IN = ("tokens", "cotangent", "w_qkv", "qv_bias", "w_out", "w_fc1", "fc1_bias", "w_fc2")
IN += ("norm_gain", "norm_bias", "layer_scale", "out_bias")
OUT = ("out_tokens", "grad_tokens", "g_qkv", "g_out", "g_fc1", "g_fc2", "g_vec", "g_shift", "g_unit")


def pair(send_recv, *at):
    return [s.at[at] for s in send_recv]


class Program:
    def __init__(self, flat):
        for name, ref in zip(IN + OUT, flat):
            setattr(self, name, ref)
        self.r = Refs(flat[len(IN + OUT) :])
        self.ring = Ring(*self.r.ring)

    def small_job(self):
        r = self.r
        return Gather("small", r.small_src, r.small, *r.small_sems)

    def head_jobs(self, l):
        r = self.r
        return (
            Gather("qkv", self.w_qkv.at[l], r.wqkv.at[l], *pair(r.qkv_sems, l)),
            Gather("out", self.w_out.at[l], r.wout.at[l], *pair(r.out_sems, l)),
        )

    def unit_jobs(self, l):
        r = self.r
        return (
            Relay("fc1", self.w_fc1.at[l], r.wfc1.at[l], *pair(r.fc1_sems, l), True),
            Relay("fc2", self.w_fc2.at[l], r.wfc2.at[l], *pair(r.fc2_sems, l), False),
        )

    def head_sums(self, l):
        r = self.r
        return (
            Scatter("qkv", r.dqkv.at[l], r.land_qkv.at[l], *pair(r.dqkv_sems, l)),
            Scatter("out", r.dout.at[l], r.land_out.at[l], *pair(r.dout_sems, l)),
        )

    def unit_sums(self, l):
        r = self.r
        return (
            Scatter("fc1", r.dfc1.at[l], r.land_fc1.at[l], *pair(r.dfc1_sems, l)),
            Scatter("fc2", r.dfc2.at[l], r.land_fc2.at[l], *pair(r.dfc2_sems, l)),
        )

    def finish_heads(self, l):
        qkv, out = self.head_sums(l)
        self.g_qkv[l] = qkv.total()
        self.g_out[l] = out.total()

    def finish_units(self, l):
        fc1, fc2 = self.unit_sums(l)
        self.g_fc1[l] = fc1.total()
        self.g_fc2[l] = fc2.total()

    def swap(self, i, src, dst):
        return Swap(src, dst, *pair(self.r.swap_sems, i))

    def run(self):
        r = self.r
        greeted = greet()
        for l in range(2):
            at = 0
            for ref in (self.norm_gain, self.norm_bias, self.layer_scale, self.out_bias):
                r.small_src[l, at : at + 2, :] = ref[l].astype(F32)
                at += 2
            bias = self.fc1_bias[...].astype(F32)[l : l + 1]
            r.small_src[l, 8:9, :] = bias[:, :128]
            r.small_src[l, 9:10, :] = bias[:, 128:]
            r.small_src[l, 10:11, :] = self.qv_bias[...].astype(F32)[l : l + 1]
            r.small_src[l, 11:16, :] = jnp.zeros((5, 128), F32)
        greeted()
        tokens = self.swap(0, self.tokens, r.start)
        tokens.start()
        self.small_job().start()
        for job in self.head_jobs(0):
            job.start()
        tokens.wait()
        r.stream[0] = r.start[...].astype(F32)
        self.small_job().wait()
        lax.fori_loop(0, 2, self.forward, 0)
        r.ending[...] = r.stream[2].astype(BF)
        self.cotangent_swap().wait()
        r.grad[...] = r.first_grad[...].astype(F32)
        lax.fori_loop(0, 2, self.backward, 0)
        r.start[...] = r.grad[...].astype(BF)
        back = self.swap(3, r.start, r.back)
        back.start()
        self.last_sums()
        self.ending_swap().wait()
        back.wait()
        self.grad_tokens[...] = r.back[...].astype(F32)

    def cotangent_swap(self):
        return self.swap(1, self.cotangent, self.r.first_grad)

    def ending_swap(self):
        return self.swap(2, self.r.ending, self.out_tokens)

    def forward(self, l, _):
        self.attn_forward(l)
        self.mlp_forward(l)
        return 0

    def backward(self, i, _):
        self.mlp_backward(1 - i)
        self.attn_backward(1 - i)
        return 0

    def attn_forward(self, l):
        r, ring = self.r, self.ring
        vec = r.small[0, l]
        normal, _ = norm_parts(r.stream[l])
        ring.set_own(r.normed.at[l, 0], (normal * vec[0:1] + vec[2:3]).astype(BF))
        bias_a, bias_b = r.small[0, l][10:11, 0:128], r.small[1, l][10:11, 0:128]
        shift = jnp.concatenate(
            [
                bias_a[:, :HD],
                bias_b[:, :HD],
                jnp.zeros((1, 128), F32),
                bias_a[:, HD:],
                bias_b[:, HD:],
            ],
            axis=1,
        )
        for job in self.head_jobs(l):
            job.wait()
        for job in self.unit_jobs(l):
            job.start()
        weights = r.wqkv[l].reshape(3 * 2 * HD, D)

        def project(who):
            at = ring.at[who]
            qkv = (dot_nt(ring.rows(who), weights) + shift).astype(BF)
            keys, values = qkv[:, 128:256], qkv[:, 256:]
            r.q[l, at] = qkv[:, :128] * 0.125
            r.k[l, at] = keys
            r.v[l, at] = values
            head = lane_head((2 * ROWS, 128))
            for h in range(2):
                r.mk[h, at] = jnp.where(head == h, keys, jnp.zeros_like(keys))
            r.turned[at] = values.astype(F32).T.astype(BF)

        ring.by_blocks(project)
        for job in self.unit_jobs(l):
            job.pump()
        pl.when(l == 0)(self.cotangent_swap().start)

        def attend(who):
            at = ring.at[who]

            def head_step(h, _):
                scores = dot_nt(r.mk[h].reshape(SEQ, 128), r.q[l, at])
                highest = jnp.max(scores, axis=0, keepdims=True)
                weights = jnp.exp(scores - highest)
                total = jnp.sum(weights, axis=0, keepdims=True)
                probs = (weights * (1.0 / total)).astype(BF)
                span = pl.ds(pl.multiple_of(h * HD, HD), HD)
                mixed = jnp.zeros((HD, 2 * ROWS), F32)
                for part in range(NX):
                    mixed = mixed + dot_nn(
                        r.turned[part, span, :],
                        probs[part * 2 * ROWS : (part + 1) * 2 * ROWS],
                    )
                r.mixt[span, :] = mixed
                r.lse[l, at, h] = highest + jnp.log(total)
                return 0

            lax.fori_loop(0, 2, head_step, 0)
            mixed = r.mixt[...].T.astype(BF)
            r.mixed[l, at] = mixed
            return dot_nn(mixed, r.wout[l].reshape(2 * HD, D))

        ring.back_by_blocks(attend)
        ring.merge(0)
        ring.merge(1)
        branch = ring.finish() + vec[6:7]
        r.branch[l, 0] = branch
        r.mid[l] = r.stream[l] + vec[4:5] * branch
        ring.drain()

    def mlp_forward(self, l):
        r, ring = self.r, self.ring
        vec = r.small[0, l]
        normal, _ = norm_parts(r.mid[l])
        ring.set_own(r.normed.at[l, 1], (normal * vec[1:2] + vec[3:4]).astype(BF))
        bias = jnp.concatenate(
            [r.small[z, l][row : row + 1, 0:128] for z in range(NZ) for row in (8, 9)], axis=1
        )
        for job in self.unit_jobs(l):
            job.wait()

        @pl.when(l == 0)
        def _():
            for job in self.head_jobs(1):
                job.start()

        def step(ch, who):
            at = ring.at[who]
            span = slice(ch * 2 * PART, (ch + 1) * 2 * PART)
            pre = dot_nn(ring.chunk(ch, who), r.wfc1[l]) + bias
            phi = 0.5 * (1.0 + lax.erf(pre * ROOT_HALF))
            hidden = (pre * phi).astype(BF)
            slope = phi + pre * INV_ROOT_TAU * jnp.exp(-0.5 * pre * pre)
            r.slope[l, at, span, :] = slope.astype(BF)
            r.hidden[l, at, span, :] = hidden
            ring.put(ch, who, dot_nn(hidden, r.wfc2[l]))

        ring.by_chunks(step)
        ring.merge(1)
        branch = ring.finish() + vec[7:8]
        r.branch[l, 1] = branch
        r.stream[l + 1] = r.mid[l] + vec[5:6] * branch
        ring.drain()

    def begin_backward(self, l, i, gath):
        r = self.r
        g = r.grad[...]
        scaled = r.small[0, l][4 + i : 5 + i] * g
        self.ring.set_own(gath, scaled.astype(BF))
        r.sums[l, i] = jnp.zeros((8, D), F32)
        r.sums[l, i, 2:3, :] = row_sum(r.branch[l, i] * g)
        r.sums[l, i, 3:4, :] = row_sum(scaled)

    def end_backward(self, l, i, stream):
        r = self.r
        back = self.ring.finish()
        normal, inverse = norm_parts(stream)
        r.sums[l, i, 0:1, :] = row_sum(back * normal)
        r.sums[l, i, 1:2, :] = row_sum(back)
        gain = r.small[0, l][i : i + 1]
        r.grad[...] += norm_backward(back, normal, inverse, gain)
        self.ring.drain()

    def mlp_backward(self, l):
        r, ring = self.r, self.ring
        gath = r.gath.at[0]
        self.begin_backward(l, 1, gath)

        def step(ch, who):
            at = ring.at[who]
            span = slice(ch * 2 * PART, (ch + 1) * 2 * PART)
            back = dot_nt(ring.chunk(ch, who), r.wfc2[l]) * r.slope[l, at, span, :].astype(F32)
            back = back.astype(BF)
            r.pre[at, span, :] = back
            ring.put(ch, who, dot_nt(back, r.wfc1[l]))

        ring.by_chunks(step)
        fc1, fc2 = self.unit_sums(l)
        r.dfc2[l] = dot_tn(
            r.hidden[l].reshape(SEQ, 512), gath[...].reshape(SEQ, D)
        ).astype(BF)
        fc2.start()
        ring.merge(1)
        r.dfc1[l] = dot_tn(
            r.normed[l, 1].reshape(SEQ, D), r.pre[...].reshape(SEQ, 512)
        ).astype(BF)
        fc1.start()
        r.sums[l, 1, 4:5, 0:512] = row_sum(r.pre[...].reshape(SEQ, 512).astype(F32))

        self.end_backward(l, 1, r.mid[l])

    def attn_backward(self, l):
        r, ring = self.r, self.ring
        gath = r.gath.at[1]
        self.begin_backward(l, 0, gath)
        head = lane_head((2 * ROWS, 128))
        for part in range(NX):
            keys, values = r.k[l, part], r.v[l, part]
            for h in range(2):
                r.mk[h, part] = jnp.where(head == h, keys, jnp.zeros_like(keys))
                r.mv[h, part] = jnp.where(head == h, values, jnp.zeros_like(values))
            r.turned[part] = keys.astype(F32).T.astype(BF)
        r.dk[...] = jnp.zeros((SEQ, 128), F32)
        r.dv[...] = jnp.zeros((SEQ, 128), F32)

        def attend(who):
            at = ring.at[who]
            if who == FAR:
                pl.when(l == 1)(self.ending_swap().start)
            r.gmix[at] = dot_nt(ring.rows(who), r.wout[l].reshape(2 * HD, D)).astype(BF)

            def head_step(h, _):
                queries, mine = r.q[l, at], r.gmix[at]
                probs = jnp.exp(dot_nt(r.mk[h].reshape(SEQ, 128), queries) - r.lse[l, at, h])
                back = dot_nt(r.mv[h].reshape(SEQ, 128), mine)
                delta = jnp.sum(probs * back, axis=0, keepdims=True)
                dscores = (probs * (back - delta)).astype(BF)
                span = pl.ds(pl.multiple_of(h * HD, HD), HD)
                turned = jnp.zeros((HD, 2 * ROWS), F32)
                for part in range(NX):
                    turned = turned + dot_nn(
                        r.turned[part, span, :],
                        dscores[part * 2 * ROWS : (part + 1) * 2 * ROWS],
                    )
                r.mixt[span, :] = turned * 0.125
                mask = head == h
                r.dk[...] += dot_nn(dscores, jnp.where(mask, queries, jnp.zeros_like(queries)))
                r.dv[...] += dot_nn(
                    probs.astype(BF), jnp.where(mask, mine, jnp.zeros_like(mine))
                )
                return 0

            lax.fori_loop(0, 2, head_step, 0)
            r.dq[at] = r.mixt[...].T.astype(BF)

        ring.by_blocks(attend)
        for part in range(NX):
            span = slice(part * 2 * ROWS, (part + 1) * 2 * ROWS)
            r.dall[part] = jnp.concatenate(
                [r.dq[part], r.dk[span, :].astype(BF), r.dv[span, :].astype(BF)], axis=1
            )
        weights = r.wqkv[l].reshape(3 * 2 * HD, D)
        ring.back_by_blocks(lambda who: dot_nn(r.dall[ring.at[who]], weights))
        qkv, out = self.head_sums(l)
        whole = r.dall[...].reshape(SEQ, 384)
        dqkv = dot_tn(whole, r.normed[l, 0].reshape(SEQ, D)).astype(BF)
        r.dqkv[l] = dqkv.reshape(3, NZ, HD, D)
        qkv.start()
        ring.merge(0)
        ring.merge(1)
        dout = dot_tn(r.mixed[l].reshape(SEQ, 128), gath[...].reshape(SEQ, D)).astype(BF)
        r.dout[l] = dout.reshape(NZ, HD, D)
        out.start()
        unit = row_sum(whole.astype(F32))
        r.sums[l, 0, 4:5, 0:256] = jnp.concatenate(
            [
                unit[:, 0:HD],
                unit[:, 256 : 256 + HD],
                unit[:, HD:128],
                unit[:, 256 + HD : 384],
            ],
            axis=1,
        )
        self.end_backward(l, 0, r.stream[l])

    def last_sums(self):
        r = self.r
        for l in range(2):
            for i in range(2):
                sums = r.sums[l, i]
                for kind in range(4):
                    row = kind * 4 + l * 2 + i
                    r.vec_src[row : row + 1, :] = sums[kind : kind + 1]
            heads, units = r.sums[l, 0], r.sums[l, 1]
            for z in range(NZ):
                for at, row in ((0, l * 2), (128, l * 2 + 1)):
                    at = at + z * 256
                    r.unit_src[z, row : row + 1, :] = units[4:5, at : at + 128]
                r.unit_src[z, 4 + l : 5 + l, :] = heads[4:5, z * 128 : (z + 1) * 128]
                r.unit_src[z, 6 + l : 7 + l, :] = jnp.zeros((1, 128), F32)
        vec = Scatter("vec", r.vec_src, r.land_vec, *r.vec_sems)
        unit = Scatter("unit", r.unit_src, r.land_unit, *r.unit_sems)
        vec.start()
        unit.start()
        self.finish_units(1)
        self.finish_heads(1)
        r.vec_sum[...] = vec.total()

        def copy(step):
            return pltpu.make_async_remote_copy(
                src_ref=r.vec_sum,
                dst_ref=r.land_ring.at[step],
                send_sem=r.ring_sems[0].at[step],
                recv_sem=r.ring_sems[1].at[step],
                device_id=ring_id(step),
                device_id_type=MESH,
            )

        for s in range(1, 2 * NX):
            copy(s).start()
        self.finish_units(0)
        units = unit.total()
        self.g_shift[...] = units[4:6]
        for l in range(2):
            self.g_unit[l : l + 1, 0:128] = units[2 * l : 2 * l + 1]
            self.g_unit[l : l + 1, 128:256] = units[2 * l + 1 : 2 * l + 2]
        self.finish_heads(0)
        total = r.vec_sum[...]
        for s in range(1, 2 * NX):
            copy(s).wait()
            total = total + r.land_ring[s]
        self.g_vec[...] = total


def whole_kernel(*flat):
    Program(flat).run()


def run_whole(*args):
    outs = [
        jax.ShapeDtypeStruct((ROWS, D), BF),
        jax.ShapeDtypeStruct((ROWS, D), F32),
        jax.ShapeDtypeStruct((2, 3, HD, 128), F32),
        jax.ShapeDtypeStruct((2, HD, 128), F32),
        jax.ShapeDtypeStruct((2, 128, 256), F32),
        jax.ShapeDtypeStruct((2, 256, 128), F32),
        jax.ShapeDtypeStruct((16, 128), F32),
        jax.ShapeDtypeStruct((2, 128), F32),
        jax.ShapeDtypeStruct((2, 256), F32),
    ]
    whole = pl.BlockSpec(memory_space=pltpu.VMEM)
    return pl.pallas_call(
        whole_kernel,
        out_shape=outs,
        in_specs=[whole] * len(args),
        out_specs=[whole] * len(outs),
        scratch_shapes=scratch_list(),
        compiler_params=pltpu.CompilerParams(
            collective_id=0, has_side_effects=True, vmem_limit_bytes=VMEM_BYTES
        ),
        cost_estimate=pl.CostEstimate(
            flops=24_000_000_000, bytes_accessed=8_000_000, transcendentals=10_000_000
        ),
    )(*args)


def on_device(
    tokens,
    cotangent,
    w_qkv,
    qv_bias,
    w_out,
    w_fc1,
    fc1_bias,
    w_fc2,
    norm_gain,
    norm_bias,
    layer_scale,
    out_bias,
):
    out_tokens, grad_tokens, g_qkv, g_out, g_fc1, g_fc2, g_vec, g_shift, g_unit = run_whole(
        tokens,
        cotangent,
        jnp.swapaxes(w_qkv[:, :, 0, :], 1, 2).reshape(2, 3, HD, 128),
        qv_bias.reshape(2, 128),
        w_out.reshape(2, HD, 128),
        w_fc1,
        fc1_bias,
        w_fc2,
        norm_gain,
        norm_bias,
        layer_scale,
        out_bias,
    )
    vec = g_vec.reshape(4, 2, 2, 128)
    return (
        out_tokens,
        grad_tokens,
        jnp.swapaxes(g_qkv.reshape(2, 3 * HD, 128), 1, 2)[:, :, None, :],
        g_shift[:, None, :],
        g_out[:, None],
        g_fc1,
        g_unit,
        g_fc2,
        vec[0],
        vec[1],
        vec[2],
        vec[3],
    )


def solution(mesh):
    split = Mesh(
        mesh.devices.reshape(mesh.shape["fsdp"], NX, NZ, 2),
        ("fsdp", "tensor_0", "tensor_1", "tensor_2"),
    )
    return jax.shard_map(
        on_device,
        mesh=split,
        in_specs=(
            P(FSDP_TENSOR, None),
            P(FSDP_TENSOR, None),
            P(None, "fsdp", TENSOR, None),
            P(None, TENSOR, None),
            P(None, TENSOR, None, "fsdp"),
            P(None, "fsdp", TENSOR),
            P(None, TENSOR),
            P(None, TENSOR, "fsdp"),
            P(None, None, "fsdp"),
            P(None, None, "fsdp"),
            P(None, None, "fsdp"),
            P(None, None, "fsdp"),
        ),
        out_specs=(
            P(FSDP_TENSOR, None),
            P(FSDP_TENSOR, None),
            P(None, "fsdp", TENSOR, None),
            P(None, TENSOR, None),
            P(None, TENSOR, None, "fsdp"),
            P(None, "fsdp", TENSOR),
            P(None, TENSOR),
            P(None, TENSOR, "fsdp"),
            P(None, None, "fsdp"),
            P(None, None, "fsdp"),
            P(None, None, "fsdp"),
            P(None, None, "fsdp"),
        ),
        check_vma=False,
    )
```

```python
import jax
import jax.numpy as jnp
from jax import lax
from jax.experimental import pallas as pl
from jax.experimental.pallas import tpu as pltpu
from jax.sharding import Mesh
from jax.sharding import PartitionSpec as P

D = 1024
HD = 64
SEQ = 1024
ROWS = 128
NX = 4
NF = 8
NZ = 2
F32 = jnp.float32
BF = jnp.bfloat16
TENSOR = ("tensor_0", "tensor_1", "tensor_2")
FSDP_TENSOR = ("fsdp", "tensor_0", "tensor_1", "tensor_2")
MESH = pl.DeviceIdType.MESH
EPS = 1e-06
ROOT_HALF = 0.7071067811865476
INV_ROOT_TAU = 0.3989422804014327
CHUNKS = 2
PART = ROWS // CHUNKS
HALF = PART // 2
GCOPIES = 10
SCOPIES = 10
TOP = pl.ds(0, HALF)
BOTTOM = pl.ds(HALF, HALF)
VMEM_BYTES = 62 * 1024 * 1024
OWN, LEFT, RIGHT, FAR = 0, 1, 2, 3


def dot_nn(left, right):
    return lax.dot_general(left, right, (((1,), (0,)), ((), ())), preferred_element_type=F32)


def dot_nt(left, right):
    return lax.dot_general(left, right, (((1,), (1,)), ((), ())), preferred_element_type=F32)


def dot_tn(left, right):
    return lax.dot_general(left, right, (((0,), (0,)), ((), ())), preferred_element_type=F32)


def norm_parts(stream):
    centre = stream - jnp.mean(stream, axis=-1, keepdims=True)
    inverse = lax.rsqrt(jnp.mean(centre * centre, axis=-1, keepdims=True) + EPS)
    return centre * inverse, inverse


def norm_backward(grad_out, normal, inverse, gain):
    scaled = grad_out * gain
    return inverse * (
        scaled
        - jnp.mean(scaled, axis=-1, keepdims=True)
        - normal * jnp.mean(scaled * normal, axis=-1, keepdims=True)
    )


def group_index():
    return lax.axis_index("fsdp"), lax.axis_index("tensor_1")


def group_peer(step):
    f, z = group_index()
    at = lax.rem(f * NZ + z + step, NF * NZ)
    return at // NZ, lax.rem(at, NZ)


def group_id(step):
    f, z = group_peer(step)
    return {"fsdp": f, "tensor_1": z}


def cols(f, width=128):
    return pl.ds(pl.multiple_of(f * width, width), width)


VIEWS = {
    "qkv": lambda ref, f, z: ref.at[:, z, :, cols(f)],
    "out": lambda ref, f, z: ref.at[z, :, cols(f)],
    "small": lambda ref, f, z: ref.at[z, :, :, cols(f)],
    "fc1": lambda ref, f, z: ref.at[cols(f), cols(z, 256)],
    "fc2": lambda ref, f, z: ref.at[cols(z, 256), cols(f)],
    "vec": lambda ref, f, z: ref.at[:, cols(f)],
    "unit": lambda ref, f, z: ref.at[z],
}


def each_peer(act):
    def step(s, _):
        act(s)
        return 0

    lax.fori_loop(1, NF * NZ, step, 0)


class Gather:
    def __init__(self, kind, src, dst, send, recv):
        self.view, self.src, self.dst = VIEWS[kind], src, dst
        self.send, self.recv = send, recv

    def copy(self, step):
        return pltpu.make_async_remote_copy(
            src_ref=self.src,
            dst_ref=self.view(self.dst, *group_index()),
            send_sem=self.send.at[step],
            recv_sem=self.recv.at[step],
            device_id=group_id(step),
            device_id_type=MESH,
        )

    def local(self):
        return pltpu.make_async_copy(
            self.src, self.view(self.dst, *group_index()), self.send.at[0]
        )

    def start(self):
        self.local().start()
        each_peer(lambda s: self.copy(s).start())

    def wait(self):
        self.local().wait()
        each_peer(lambda s: self.copy(s).wait())


class Relay:
    def __init__(self, kind, src, dst, send, recv, y_first):
        self.view, self.src, self.dst = VIEWS[kind], src, dst
        self.send, self.recv, self.y_first = send, recv, y_first
        f, z = group_index()
        self.y, self.z = f // 2, z * 2 + lax.rem(f, 2)

    def place(self, first, second):
        y, z = (first, second) if self.y_first else (second, first)
        y, z = lax.rem(self.y + y, 4), lax.rem(self.z + z, 4)
        return y * 2 + lax.rem(z, 2), z // 2

    def copy(self, first, second):
        if second:
            f, z = self.place(0, second)
            origin = self.place(4 - first if first else 0, 0)
        else:
            f, z = self.place(first, 0)
            origin = self.place(0, 0)
        there = self.view(self.dst, *origin)
        return pltpu.make_async_remote_copy(
            src_ref=there if first and second else self.src,
            dst_ref=there,
            send_sem=self.send.at[first * 4 + second],
            recv_sem=self.recv.at[first * 4 + second],
            device_id={"fsdp": f, "tensor_1": z},
            device_id_type=MESH,
        )

    def local(self):
        return pltpu.make_async_copy(
            self.src, self.view(self.dst, *self.place(0, 0)), self.send.at[0]
        )

    def start(self):
        self.local().start()
        for step in (2, 1, 3):
            self.copy(step, 0).start()
        for step in (2, 1, 3):
            self.copy(0, step).start()

    def pump(self):
        for first in (1, 3, 2):
            self.copy(first, 0).wait_recv()
            for second in (2, 1, 3):
                self.copy(first, second).start()

    def wait(self):
        self.local().wait()
        for first in range(1, 4):
            self.copy(first, 0).wait_send()
        for first in range(4):
            for second in range(1, 4):
                self.copy(first, second).wait()


class Scatter:
    def __init__(self, kind, src, land, send, recv):
        self.view, self.src, self.land = VIEWS[kind], src, land
        self.send, self.recv = send, recv

    def copy(self, step):
        return pltpu.make_async_remote_copy(
            src_ref=self.view(self.src, *group_peer(step)),
            dst_ref=self.land.at[step],
            send_sem=self.send.at[step],
            recv_sem=self.recv.at[step],
            device_id=group_id(step),
            device_id_type=MESH,
        )

    def local(self):
        return pltpu.make_async_copy(
            self.view(self.src, *group_index()), self.land.at[0], self.send.at[0]
        )

    def start(self):
        self.local().start()
        each_peer(lambda s: self.copy(s).start())

    def total(self):
        self.local().wait()
        each_peer(lambda s: self.copy(s).wait())
        return sum(self.land[s].astype(F32) for s in range(NF * NZ))


class Swap:
    def __init__(self, src, dst, send, recv):
        x, z = lax.axis_index("tensor_0"), lax.axis_index("tensor_1")
        self.moves = lax.rem(x // 2 + z, 2) == 1
        self.remote = pltpu.make_async_remote_copy(
            src_ref=src,
            dst_ref=dst,
            send_sem=send,
            recv_sem=recv,
            device_id=swap_id(),
            device_id_type=MESH,
        )
        self.stay = pltpu.make_async_copy(src, dst, send)

    def start(self):
        pl.when(self.moves)(self.remote.start)
        pl.when(jnp.logical_not(self.moves))(self.stay.start)

    def wait(self):
        pl.when(self.moves)(self.remote.wait)
        pl.when(jnp.logical_not(self.moves))(self.stay.wait)


def swap_id():
    x, z = lax.axis_index("tensor_0"), lax.axis_index("tensor_1")
    return {"tensor_0": lax.rem(x + 2, NX), "tensor_1": 1 - z}


def ring_id(step):
    x, c = lax.axis_index("tensor_0"), lax.axis_index("tensor_2")
    at = lax.rem(x * 2 + c + step, 2 * NX)
    return {"tensor_0": at // 2, "tensor_2": lax.rem(at, 2)}


def greet():
    barrier = pltpu.get_barrier_semaphore()

    def signal(where):
        pl.semaphore_signal(barrier, inc=1, device_id=where, device_id_type=MESH)

    for s in range(1, 2 * NX):
        signal(ring_id(s))
    signal(swap_id())
    each_peer(lambda s: signal(group_id(s)))
    return lambda: pl.semaphore_wait(barrier, 2 * NX + NF * NZ - 1)


class Ring:
    def __init__(self, part, pin, sout, rin, held, gsend, grecv, ssend, srecv):
        self.x, self.c = lax.axis_index("tensor_0"), lax.axis_index("tensor_2")
        self.at = [self.x] + [lax.rem(self.x + s, NX) for s in (3, 1, 2)]
        self.part, self.pin = part, pin
        self.sout, self.rin, self.held = sout, rin, held
        self.gsend, self.grecv, self.ssend, self.srecv = gsend, grecv, ssend, srecv
        self.left = {"tensor_0": self.at[LEFT]}
        self.right = {"tensor_0": self.at[RIGHT]}
        self.twin = {"tensor_2": 1 - self.c}

    def gcopy(self, ch, i):
        who, rows, to = (
            (OWN, None, self.twin),
            (OWN, TOP, self.right),
            (OWN, BOTTOM, self.right),
            (OWN, BOTTOM, self.left),
            (OWN, TOP, self.left),
            (LEFT, TOP, self.right),
            (RIGHT, BOTTOM, self.left),
            (LEFT, None, self.twin),
            (RIGHT, None, self.twin),
            (FAR, None, self.twin),
        )[i]
        ref = self.gath.at[self.at[who], ch, self.c]
        if rows is not None:
            ref = ref.at[rows]
        return pltpu.make_async_remote_copy(
            src_ref=ref,
            dst_ref=ref,
            send_sem=self.gsend.at[ch * GCOPIES + i],
            recv_sem=self.grecv.at[ch * GCOPIES + i],
            device_id=to,
            device_id_type=MESH,
        )

    def got(self, ch, i):
        self.gcopy(ch, i).wait_recv()

    def go(self, ch, *which):
        for i in which:
            self.gcopy(ch, i).start()

    def set_own(self, gath, rows):
        self.gath = gath
        for ch in range(CHUNKS):
            gath[self.x, ch, self.c] = rows[ch * PART : (ch + 1) * PART]
        for ch in range(CHUNKS):
            self.go(ch, 1, 3, 2, 4, 0)

    def near(self, ch):
        self.relay(ch)
        self.pass_on(ch)

    def relay(self, ch):
        self.got(ch, 1)
        self.go(ch, 5)
        self.got(ch, 3)
        self.go(ch, 6)

    def pass_on(self, ch):
        self.got(ch, 2)
        self.go(ch, 7)
        self.got(ch, 4)
        self.go(ch, 8)

    def far(self, ch):
        self.got(ch, 5)
        self.got(ch, 6)
        self.go(ch, 9)

    def arrive(self, ch, who):
        self.got(ch, (0, 7, 8, 9)[who])

    def arrive_both(self, who):
        self.arrive(0, who)
        self.arrive(1, who)

    def chunk(self, ch, who):
        return self.gath[self.at[who], ch].reshape(2 * PART, D)

    def rows(self, who):
        return self.gath[self.at[who]].reshape(2 * ROWS, D)

    def pcopy(self, ch, who):
        return pltpu.make_async_remote_copy(
            src_ref=self.part.at[ch, who, 1 - self.c],
            dst_ref=self.pin.at[ch, who],
            send_sem=self.ssend.at[ch * SCOPIES + 6 + who],
            recv_sem=self.srecv.at[ch * SCOPIES + 6 + who],
            device_id=self.twin,
            device_id_type=MESH,
        )

    def scopy(self, ch, i):
        return pltpu.make_async_remote_copy(
            src_ref=self.sout.at[ch, i],
            dst_ref=self.rin.at[ch, i],
            send_sem=self.ssend.at[ch * SCOPIES + i],
            recv_sem=self.srecv.at[ch * SCOPIES + i],
            device_id=self.left if i in (1, 4, 5) else self.right,
            device_id_type=MESH,
        )

    def put(self, ch, who, value):
        self.part[ch, who] = value.astype(BF).reshape(2, PART, D)
        self.pcopy(ch, who).start()

    def put_both(self, who, value):
        self.put(0, who, value[: 2 * PART])
        self.put(1, who, value[2 * PART :])

    def send(self, ch, i, value):
        self.sout[ch, i] = value.astype(BF)
        self.scopy(ch, i).start()

    def both_cores(self, ch, who):
        self.pcopy(ch, who).wait_recv()
        return self.part[ch, who, self.c].astype(F32) + self.pin[ch, who].astype(F32)

    def flush(self, ch, who):
        total = self.both_cores(ch, who)
        if who == FAR:
            self.send(ch, 0, total[:HALF])
            self.send(ch, 1, total[HALF:])
        elif who == RIGHT:
            self.send(ch, 2, total[HALF:])
            self.held[ch, 0] = total[:HALF]
        else:
            self.send(ch, 4, total[:HALF])
            self.held[ch, 1] = total[HALF:]

    def flush_both(self, *which):
        for who in which:
            for ch in range(CHUNKS):
                self.flush(ch, who)

    def merge(self, ch):
        self.scopy(ch, 0).wait_recv()
        self.send(ch, 3, self.held[ch, 0] + self.rin[ch, 0].astype(F32))
        self.scopy(ch, 1).wait_recv()
        self.send(ch, 5, self.held[ch, 1] + self.rin[ch, 1].astype(F32))

    def finish(self):
        for ch in range(CHUNKS):
            for i in range(GCOPIES):
                self.gcopy(ch, i).wait_send()
        rows = []
        for ch in range(CHUNKS):
            total = self.both_cores(ch, OWN)
            for i in (2, 4, 3, 5):
                self.scopy(ch, i).wait_recv()
            rin = [self.rin[ch, i].astype(F32) for i in (2, 3, 4, 5)]
            rows += [total[:HALF] + rin[1] + rin[2], total[HALF:] + rin[0] + rin[3]]
        return jnp.concatenate(rows, axis=0)

    def drain(self):
        for ch in range(CHUNKS):
            for i in range(6):
                self.scopy(ch, i).wait_send()
            for i in range(4):
                self.pcopy(ch, i).wait_send()

    def by_chunks(self, step):
        self.arrive(0, OWN)
        step(0, OWN)
        self.near(0)
        self.arrive(1, OWN)
        step(1, OWN)
        for who in (LEFT, RIGHT):
            self.arrive(0, who)
            step(0, who)
        self.near(1)
        self.flush(0, LEFT)
        self.flush(0, RIGHT)
        self.far(0)
        self.arrive(1, LEFT)
        step(1, LEFT)
        self.arrive(0, FAR)
        step(0, FAR)
        self.far(1)
        self.arrive(1, RIGHT)
        step(1, RIGHT)
        self.flush(0, FAR)
        self.arrive(1, FAR)
        step(1, FAR)
        self.flush(1, LEFT)
        self.flush(1, RIGHT)
        self.flush(1, FAR)
        self.merge(0)

    def by_blocks(self, step):
        self.arrive_both(OWN)
        step(OWN)
        self.near(0)
        self.near(1)
        self.arrive_both(LEFT)
        step(LEFT)
        self.far(0)
        self.far(1)
        self.arrive_both(RIGHT)
        step(RIGHT)
        self.arrive_both(FAR)
        step(FAR)

    def by_pairs(self, step):
        self.arrive_both(OWN)
        step((OWN, 0), (OWN, 1))
        self.near(0)
        self.relay(1)
        self.arrive(0, LEFT)
        self.arrive(0, RIGHT)
        step((LEFT, 0), (RIGHT, 0))
        self.pass_on(1)
        self.far(0)
        self.far(1)
        self.arrive(1, LEFT)
        self.arrive(1, RIGHT)
        step((LEFT, 1), (RIGHT, 1))
        self.arrive_both(FAR)
        step((FAR, 0), (FAR, 1))

    def back_by_blocks(self, value):
        for who in (FAR, LEFT, RIGHT, OWN):
            self.put_both(who, value(who))
            if who == LEFT:
                self.flush_both(FAR)
            elif who == RIGHT:
                self.flush_both(LEFT, RIGHT)


RING_SCRATCH = [
    pltpu.VMEM((CHUNKS, NX, 2, PART, D), BF),
    pltpu.VMEM((CHUNKS, NX, PART, D), BF),
    pltpu.VMEM((CHUNKS, 6, HALF, D), BF),
    pltpu.VMEM((CHUNKS, 6, HALF, D), BF),
    pltpu.VMEM((CHUNKS, 2, HALF, D), F32),
    pltpu.SemaphoreType.DMA((CHUNKS * GCOPIES,)),
    pltpu.SemaphoreType.DMA((CHUNKS * GCOPIES,)),
    pltpu.SemaphoreType.DMA((CHUNKS * SCOPIES,)),
    pltpu.SemaphoreType.DMA((CHUNKS * SCOPIES,)),
]


def lane_head(shape):
    return lax.broadcasted_iota(jnp.int32, shape, len(shape) - 1) // HD


def span_of(half):
    return slice(half * 2 * PART, (half + 1) * 2 * PART)


def row_sum(value):
    return jnp.sum(value, axis=0, keepdims=True)


PIECE = {
    "qkv": (3, HD, 128),
    "out": (HD, 128),
    "fc1": (128, 256),
    "fc2": (256, 128),
    "vec": (16, 128),
    "unit": (8, 128),
}
HEADS = (NX, 2 * ROWS, 128)


def sems(*shape):
    return [pltpu.SemaphoreType.DMA(shape)] * 2


SCRATCH = dict(
    small_src=pltpu.VMEM((2, 16, 128), F32),
    small=pltpu.VMEM((NZ, 2, 16, D), F32),
    wqkv=pltpu.VMEM((2, 3, NZ, HD, D), BF),
    wout=pltpu.VMEM((2, NZ, HD, D), BF),
    wfc1=pltpu.VMEM((2, D, 512), BF),
    wfc2=pltpu.VMEM((2, 512, D), BF),
    start=pltpu.VMEM((ROWS, D), BF),
    first_grad=pltpu.VMEM((ROWS, D), BF),
    ending=pltpu.VMEM((ROWS, D), BF),
    back=pltpu.VMEM((ROWS, D), BF),
    stream=pltpu.VMEM((3, ROWS, D), F32),
    mid=pltpu.VMEM((2, ROWS, D), F32),
    branch=pltpu.VMEM((2, 2, ROWS, D), F32),
    grad=pltpu.VMEM((ROWS, D), F32),
    normed=pltpu.VMEM((2, 2, NX, CHUNKS, 2, PART, D), BF),
    q=pltpu.VMEM((2, *HEADS), BF),
    k=pltpu.VMEM((2, *HEADS), BF),
    v=pltpu.VMEM((2, *HEADS), BF),
    mixed=pltpu.VMEM((2, *HEADS), BF),
    lse=pltpu.VMEM((2, NX, 2, 1, 2 * ROWS), F32),
    hidden=pltpu.VMEM((2, NX, 2 * ROWS, 512), BF),
    slope=pltpu.VMEM((2, NX, 2 * ROWS, 512), BF),
    mk=pltpu.VMEM((2, *HEADS), BF),
    mv=pltpu.VMEM((2, *HEADS), BF),
    turned=pltpu.VMEM((NX, 128, 2 * ROWS), BF),
    mixt=pltpu.VMEM((128, 2 * ROWS), F32),
    gath=pltpu.VMEM((2, NX, CHUNKS, 2, PART, D), BF),
    pre=pltpu.VMEM((NX, 2 * ROWS, 512), BF),
    gmix=pltpu.VMEM((2 * ROWS, 128), BF),
    qmix=pltpu.VMEM((2 * ROWS, 128), BF),
    lmix=pltpu.VMEM((2, 1, 2 * ROWS), F32),
    dq=pltpu.VMEM(HEADS, BF),
    dk=pltpu.VMEM((SEQ, 128), F32),
    dv=pltpu.VMEM((SEQ, 128), F32),
    dall=pltpu.VMEM((NX, 2 * ROWS, 384), BF),
    sums=pltpu.VMEM((2, 2, 8, D), F32),
    dqkv=pltpu.VMEM((2, 3, NZ, HD, D), BF),
    dout=pltpu.VMEM((2, NZ, HD, D), BF),
    dfc1=pltpu.VMEM((2, D, 512), BF),
    dfc2=pltpu.VMEM((2, 512, D), BF),
    vec_src=pltpu.VMEM((16, D), F32),
    unit_src=pltpu.VMEM((NZ, 8, 128), F32),
    vec_sum=pltpu.VMEM((16, 128), F32),
    land_qkv=pltpu.VMEM((2, NF * NZ, *PIECE["qkv"]), BF),
    land_out=pltpu.VMEM((2, NF * NZ, *PIECE["out"]), BF),
    land_fc1=pltpu.VMEM((2, NF * NZ, *PIECE["fc1"]), BF),
    land_fc2=pltpu.VMEM((2, NF * NZ, *PIECE["fc2"]), BF),
    land_vec=pltpu.VMEM((NF * NZ, *PIECE["vec"]), F32),
    land_unit=pltpu.VMEM((NF * NZ, *PIECE["unit"]), F32),
    land_ring=pltpu.VMEM((2 * NX, *PIECE["vec"]), F32),
    small_sems=sems(NF * NZ),
    qkv_sems=sems(2, NF * NZ),
    out_sems=sems(2, NF * NZ),
    fc1_sems=sems(2, NF * NZ),
    fc2_sems=sems(2, NF * NZ),
    dqkv_sems=sems(2, NF * NZ),
    dout_sems=sems(2, NF * NZ),
    dfc1_sems=sems(2, NF * NZ),
    dfc2_sems=sems(2, NF * NZ),
    vec_sems=sems(NF * NZ),
    unit_sems=sems(NF * NZ),
    swap_sems=sems(4),
    ring_sems=sems(2 * NX),
    ring=RING_SCRATCH,
)


def scratch_list():
    flat = []
    for item in SCRATCH.values():
        flat += item if isinstance(item, list) else [item]
    return flat


class Refs:
    def __init__(self, flat):
        flat = list(flat)
        for name, item in SCRATCH.items():
            if isinstance(item, list):
                setattr(self, name, [flat.pop(0) for _ in item])
            else:
                setattr(self, name, flat.pop(0))


IN = ("tokens", "cotangent", "w_qkv", "qv_bias", "w_out", "w_fc1", "fc1_bias", "w_fc2")
IN += ("norm_gain", "norm_bias", "layer_scale", "out_bias")
OUT = ("out_tokens", "grad_tokens", "g_qkv", "g_out", "g_fc1", "g_fc2", "g_vec", "g_shift", "g_unit")


def pair(send_recv, *at):
    return [s.at[at] for s in send_recv]


class Program:
    def __init__(self, flat):
        for name, ref in zip(IN + OUT, flat):
            setattr(self, name, ref)
        self.r = Refs(flat[len(IN + OUT) :])
        self.ring = Ring(*self.r.ring)

    def small_job(self):
        r = self.r
        return Gather("small", r.small_src, r.small, *r.small_sems)

    def head_jobs(self, l):
        r = self.r
        return (
            Gather("qkv", self.w_qkv.at[l], r.wqkv.at[l], *pair(r.qkv_sems, l)),
            Gather("out", self.w_out.at[l], r.wout.at[l], *pair(r.out_sems, l)),
        )

    def unit_jobs(self, l):
        r = self.r
        return (
            Relay("fc1", self.w_fc1.at[l], r.wfc1.at[l], *pair(r.fc1_sems, l), True),
            Relay("fc2", self.w_fc2.at[l], r.wfc2.at[l], *pair(r.fc2_sems, l), False),
        )

    def head_sums(self, l):
        r = self.r
        return (
            Scatter("qkv", r.dqkv.at[l], r.land_qkv.at[l], *pair(r.dqkv_sems, l)),
            Scatter("out", r.dout.at[l], r.land_out.at[l], *pair(r.dout_sems, l)),
        )

    def unit_sums(self, l):
        r = self.r
        return (
            Scatter("fc1", r.dfc1.at[l], r.land_fc1.at[l], *pair(r.dfc1_sems, l)),
            Scatter("fc2", r.dfc2.at[l], r.land_fc2.at[l], *pair(r.dfc2_sems, l)),
        )

    def finish_heads(self, l):
        qkv, out = self.head_sums(l)
        self.g_qkv[l] = qkv.total()
        self.g_out[l] = out.total()

    def finish_units(self, l):
        fc1, fc2 = self.unit_sums(l)
        self.g_fc1[l] = fc1.total()
        self.g_fc2[l] = fc2.total()

    def swap(self, i, src, dst):
        return Swap(src, dst, *pair(self.r.swap_sems, i))

    def run(self):
        r = self.r
        greeted = greet()
        for l in range(2):
            at = 0
            for ref in (self.norm_gain, self.norm_bias, self.layer_scale, self.out_bias):
                r.small_src[l, at : at + 2, :] = ref[l].astype(F32)
                at += 2
            bias = self.fc1_bias[...].astype(F32)[l : l + 1]
            r.small_src[l, 8:9, :] = bias[:, :128]
            r.small_src[l, 9:10, :] = bias[:, 128:]
            r.small_src[l, 10:11, :] = self.qv_bias[...].astype(F32)[l : l + 1]
            r.small_src[l, 11:16, :] = jnp.zeros((5, 128), F32)
        greeted()
        tokens = self.swap(0, self.tokens, r.start)
        tokens.start()
        self.small_job().start()
        for job in self.head_jobs(0):
            job.start()
        tokens.wait()
        r.stream[0] = r.start[...].astype(F32)
        self.small_job().wait()
        lax.fori_loop(0, 2, self.forward, 0)
        r.ending[...] = r.stream[2].astype(BF)
        self.cotangent_swap().wait()
        r.grad[...] = r.first_grad[...].astype(F32)
        lax.fori_loop(0, 2, self.backward, 0)
        r.start[...] = r.grad[...].astype(BF)
        back = self.swap(3, r.start, r.back)
        back.start()
        self.ring.drain()
        self.last_sums()
        self.ending_swap().wait()
        back.wait()
        self.grad_tokens[...] = r.back[...].astype(F32)

    def cotangent_swap(self):
        return self.swap(1, self.cotangent, self.r.first_grad)

    def ending_swap(self):
        return self.swap(2, self.r.ending, self.out_tokens)

    def forward(self, l, _):
        self.attn_forward(l)
        self.mlp_forward(l)
        return 0

    def backward(self, i, _):
        self.mlp_backward(1 - i)
        self.attn_backward(1 - i)
        return 0

    def attn_forward(self, l):
        r, ring = self.r, self.ring
        vec = r.small[0, l]
        normal, _ = norm_parts(r.stream[l])
        ring.set_own(r.normed.at[l, 0], (normal * vec[0:1] + vec[2:3]).astype(BF))
        pl.when(l > 0)(ring.drain)
        bias_a, bias_b = r.small[0, l][10:11, 0:128], r.small[1, l][10:11, 0:128]
        shift = jnp.concatenate(
            [
                bias_a[:, :HD],
                bias_b[:, :HD],
                jnp.zeros((1, 128), F32),
                bias_a[:, HD:],
                bias_b[:, HD:],
            ],
            axis=1,
        )
        for job in self.head_jobs(l):
            job.wait()
        for job in self.unit_jobs(l):
            job.start()
        weights = r.wqkv[l].reshape(3 * 2 * HD, D)

        def project(who):
            at = ring.at[who]
            qkv = (dot_nt(ring.rows(who), weights) + shift).astype(BF)
            keys, values = qkv[:, 128:256], qkv[:, 256:]
            r.q[l, at] = qkv[:, :128] * 0.125
            r.k[l, at] = keys
            r.v[l, at] = values
            head = lane_head((2 * ROWS, 128))
            for h in range(2):
                r.mk[h, at] = jnp.where(head == h, keys, jnp.zeros_like(keys))
            r.turned[at] = values.astype(F32).T.astype(BF)

        ring.by_blocks(project)
        for job in self.unit_jobs(l):
            job.pump()
        pl.when(l == 0)(self.cotangent_swap().start)

        def attend(who):
            at = ring.at[who]

            def head_step(h, _):
                scores = dot_nt(r.mk[h].reshape(SEQ, 128), r.q[l, at])
                highest = jnp.max(scores, axis=0, keepdims=True)
                weights = jnp.exp(scores - highest)
                total = jnp.sum(weights, axis=0, keepdims=True)
                probs = (weights * (1.0 / total)).astype(BF)
                span = pl.ds(pl.multiple_of(h * HD, HD), HD)
                mixed = jnp.zeros((HD, 2 * ROWS), F32)
                for part in range(NX):
                    mixed = mixed + dot_nn(
                        r.turned[part, span, :],
                        probs[part * 2 * ROWS : (part + 1) * 2 * ROWS],
                    )
                r.mixt[span, :] = mixed
                r.lse[l, at, h] = highest + jnp.log(total)
                return 0

            lax.fori_loop(0, 2, head_step, 0)
            mixed = r.mixt[...].T.astype(BF)
            r.mixed[l, at] = mixed
            return dot_nn(mixed, r.wout[l].reshape(2 * HD, D))

        ring.back_by_blocks(attend)
        ring.merge(0)
        ring.merge(1)
        branch = ring.finish() + vec[6:7]
        r.branch[l, 0] = branch
        r.mid[l] = r.stream[l] + vec[4:5] * branch

    def mlp_forward(self, l):
        r, ring = self.r, self.ring
        vec = r.small[0, l]
        normal, _ = norm_parts(r.mid[l])
        ring.set_own(r.normed.at[l, 1], (normal * vec[1:2] + vec[3:4]).astype(BF))
        ring.drain()
        bias = jnp.concatenate(
            [r.small[z, l][row : row + 1, 0:128] for z in range(NZ) for row in (8, 9)], axis=1
        )
        for job in self.unit_jobs(l):
            job.wait()

        @pl.when(l == 0)
        def _():
            for job in self.head_jobs(1):
                job.start()

        def step(ch, who):
            at = ring.at[who]
            span = slice(ch * 2 * PART, (ch + 1) * 2 * PART)
            pre = dot_nn(ring.chunk(ch, who), r.wfc1[l]) + bias
            phi = 0.5 * (1.0 + lax.erf(pre * ROOT_HALF))
            hidden = (pre * phi).astype(BF)
            slope = phi + pre * INV_ROOT_TAU * jnp.exp(-0.5 * pre * pre)
            r.slope[l, at, span, :] = slope.astype(BF)
            r.hidden[l, at, span, :] = hidden
            ring.put(ch, who, dot_nn(hidden, r.wfc2[l]))

        ring.by_chunks(step)
        ring.merge(1)
        branch = ring.finish() + vec[7:8]
        r.branch[l, 1] = branch
        r.stream[l + 1] = r.mid[l] + vec[5:6] * branch

    def begin_backward(self, l, i, gath):
        r = self.r
        g = r.grad[...]
        scaled = r.small[0, l][4 + i : 5 + i] * g
        self.ring.set_own(gath, scaled.astype(BF))
        self.ring.drain()
        r.sums[l, i] = jnp.zeros((8, D), F32)
        r.sums[l, i, 2:3, :] = row_sum(r.branch[l, i] * g)
        r.sums[l, i, 3:4, :] = row_sum(scaled)

    def end_backward(self, l, i, stream):
        r = self.r
        back = self.ring.finish()
        normal, inverse = norm_parts(stream)
        r.sums[l, i, 0:1, :] = row_sum(back * normal)
        r.sums[l, i, 1:2, :] = row_sum(back)
        gain = r.small[0, l][i : i + 1]
        r.grad[...] += norm_backward(back, normal, inverse, gain)

    def mlp_backward(self, l):
        r, ring = self.r, self.ring
        gath = r.gath.at[0]
        self.begin_backward(l, 1, gath)

        def step(ch, who):
            at = ring.at[who]
            span = slice(ch * 2 * PART, (ch + 1) * 2 * PART)
            back = dot_nt(ring.chunk(ch, who), r.wfc2[l]) * r.slope[l, at, span, :].astype(F32)
            back = back.astype(BF)
            r.pre[at, span, :] = back
            ring.put(ch, who, dot_nt(back, r.wfc1[l]))

        ring.by_chunks(step)
        fc1, fc2 = self.unit_sums(l)
        r.dfc2[l] = dot_tn(
            r.hidden[l].reshape(SEQ, 512), gath[...].reshape(SEQ, D)
        ).astype(BF)
        fc2.start()
        ring.merge(1)
        r.dfc1[l] = dot_tn(
            r.normed[l, 1].reshape(SEQ, D), r.pre[...].reshape(SEQ, 512)
        ).astype(BF)
        fc1.start()
        r.sums[l, 1, 4:5, 0:512] = row_sum(r.pre[...].reshape(SEQ, 512).astype(F32))

        self.end_backward(l, 1, r.mid[l])

    def attn_backward(self, l):
        r, ring = self.r, self.ring
        gath = r.gath.at[1]
        self.begin_backward(l, 0, gath)
        head = lane_head((2 * ROWS, 128))
        for part in range(NX):
            keys, values = r.k[l, part], r.v[l, part]
            for h in range(2):
                r.mk[h, part] = jnp.where(head == h, keys, jnp.zeros_like(keys))
                r.mv[h, part] = jnp.where(head == h, values, jnp.zeros_like(values))
            r.turned[part] = keys.astype(F32).T.astype(BF)
        r.dk[...] = jnp.zeros((SEQ, 128), F32)
        r.dv[...] = jnp.zeros((SEQ, 128), F32)

        def attend(*halves):
            if halves[0][0] == FAR:
                pl.when(l == 1)(self.ending_swap().start)
            at = [ring.at[who] for who, _ in halves]
            span = [slice(ch * 2 * PART, (ch + 1) * 2 * PART) for _, ch in halves]
            rows = jnp.concatenate([ring.chunk(ch, who) for who, ch in halves], axis=0)
            r.gmix[...] = dot_nt(rows, r.wout[l].reshape(2 * HD, D)).astype(BF)
            for i in range(2):
                r.qmix[span_of(i), :] = r.q[l, at[i], span[i], :]
            for h in range(2):
                r.lmix[h] = jnp.concatenate(
                    [r.lse[l, at[i], h][:, span[i]] for i in range(2)], axis=1
                )

            def head_step(h, _):
                queries, mine = r.qmix[...], r.gmix[...]
                probs = jnp.exp(dot_nt(r.mk[h].reshape(SEQ, 128), queries) - r.lmix[h])
                back = dot_nt(r.mv[h].reshape(SEQ, 128), mine)
                delta = jnp.sum(probs * back, axis=0, keepdims=True)
                dscores = (probs * (back - delta)).astype(BF)
                span = pl.ds(pl.multiple_of(h * HD, HD), HD)
                turned = jnp.zeros((HD, 2 * ROWS), F32)
                for part in range(NX):
                    turned = turned + dot_nn(
                        r.turned[part, span, :],
                        dscores[part * 2 * ROWS : (part + 1) * 2 * ROWS],
                    )
                r.mixt[span, :] = turned * 0.125
                mask = head == h
                r.dk[...] += dot_nn(dscores, jnp.where(mask, queries, jnp.zeros_like(queries)))
                r.dv[...] += dot_nn(
                    probs.astype(BF), jnp.where(mask, mine, jnp.zeros_like(mine))
                )
                return 0

            lax.fori_loop(0, 2, head_step, 0)
            turned = r.mixt[...].T.astype(BF)
            for i in range(2):
                r.dq[at[i], span[i], :] = turned[span_of(i)]

        ring.by_pairs(attend)
        for part in range(NX):
            span = slice(part * 2 * ROWS, (part + 1) * 2 * ROWS)
            r.dall[part] = jnp.concatenate(
                [r.dq[part], r.dk[span, :].astype(BF), r.dv[span, :].astype(BF)], axis=1
            )
        weights = r.wqkv[l].reshape(3 * 2 * HD, D)
        ring.back_by_blocks(lambda who: dot_nn(r.dall[ring.at[who]], weights))
        qkv, out = self.head_sums(l)
        whole = r.dall[...].reshape(SEQ, 384)
        dqkv = dot_tn(whole, r.normed[l, 0].reshape(SEQ, D)).astype(BF)
        r.dqkv[l] = dqkv.reshape(3, NZ, HD, D)
        qkv.start()
        ring.merge(0)
        ring.merge(1)
        dout = dot_tn(r.mixed[l].reshape(SEQ, 128), gath[...].reshape(SEQ, D)).astype(BF)
        r.dout[l] = dout.reshape(NZ, HD, D)
        out.start()
        unit = row_sum(whole.astype(F32))
        r.sums[l, 0, 4:5, 0:256] = jnp.concatenate(
            [
                unit[:, 0:HD],
                unit[:, 256 : 256 + HD],
                unit[:, HD:128],
                unit[:, 256 + HD : 384],
            ],
            axis=1,
        )
        self.end_backward(l, 0, r.stream[l])

    def last_sums(self):
        r = self.r
        for l in range(2):
            for i in range(2):
                sums = r.sums[l, i]
                for kind in range(4):
                    row = kind * 4 + l * 2 + i
                    r.vec_src[row : row + 1, :] = sums[kind : kind + 1]
            heads, units = r.sums[l, 0], r.sums[l, 1]
            for z in range(NZ):
                for at, row in ((0, l * 2), (128, l * 2 + 1)):
                    at = at + z * 256
                    r.unit_src[z, row : row + 1, :] = units[4:5, at : at + 128]
                r.unit_src[z, 4 + l : 5 + l, :] = heads[4:5, z * 128 : (z + 1) * 128]
                r.unit_src[z, 6 + l : 7 + l, :] = jnp.zeros((1, 128), F32)
        vec = Scatter("vec", r.vec_src, r.land_vec, *r.vec_sems)
        unit = Scatter("unit", r.unit_src, r.land_unit, *r.unit_sems)
        vec.start()
        unit.start()
        self.finish_units(1)
        self.finish_heads(1)
        r.vec_sum[...] = vec.total()

        def copy(step):
            return pltpu.make_async_remote_copy(
                src_ref=r.vec_sum,
                dst_ref=r.land_ring.at[step],
                send_sem=r.ring_sems[0].at[step],
                recv_sem=r.ring_sems[1].at[step],
                device_id=ring_id(step),
                device_id_type=MESH,
            )

        for s in range(1, 2 * NX):
            copy(s).start()
        self.finish_units(0)
        units = unit.total()
        self.g_shift[...] = units[4:6]
        for l in range(2):
            self.g_unit[l : l + 1, 0:128] = units[2 * l : 2 * l + 1]
            self.g_unit[l : l + 1, 128:256] = units[2 * l + 1 : 2 * l + 2]
        self.finish_heads(0)
        total = r.vec_sum[...]
        for s in range(1, 2 * NX):
            copy(s).wait()
            total = total + r.land_ring[s]
        self.g_vec[...] = total


def whole_kernel(*flat):
    Program(flat).run()


def run_whole(*args):
    outs = [
        jax.ShapeDtypeStruct((ROWS, D), BF),
        jax.ShapeDtypeStruct((ROWS, D), F32),
        jax.ShapeDtypeStruct((2, 3, HD, 128), F32),
        jax.ShapeDtypeStruct((2, HD, 128), F32),
        jax.ShapeDtypeStruct((2, 128, 256), F32),
        jax.ShapeDtypeStruct((2, 256, 128), F32),
        jax.ShapeDtypeStruct((16, 128), F32),
        jax.ShapeDtypeStruct((2, 128), F32),
        jax.ShapeDtypeStruct((2, 256), F32),
    ]
    whole = pl.BlockSpec(memory_space=pltpu.VMEM)
    return pl.pallas_call(
        whole_kernel,
        out_shape=outs,
        in_specs=[whole] * len(args),
        out_specs=[whole] * len(outs),
        scratch_shapes=scratch_list(),
        compiler_params=pltpu.CompilerParams(
            collective_id=0, has_side_effects=True, vmem_limit_bytes=VMEM_BYTES
        ),
        cost_estimate=pl.CostEstimate(
            flops=24_000_000_000, bytes_accessed=8_000_000, transcendentals=10_000_000
        ),
    )(*args)


def on_device(
    tokens,
    cotangent,
    w_qkv,
    qv_bias,
    w_out,
    w_fc1,
    fc1_bias,
    w_fc2,
    norm_gain,
    norm_bias,
    layer_scale,
    out_bias,
):
    out_tokens, grad_tokens, g_qkv, g_out, g_fc1, g_fc2, g_vec, g_shift, g_unit = run_whole(
        tokens,
        cotangent,
        jnp.swapaxes(w_qkv[:, :, 0, :], 1, 2).reshape(2, 3, HD, 128),
        qv_bias.reshape(2, 128),
        w_out.reshape(2, HD, 128),
        w_fc1,
        fc1_bias,
        w_fc2,
        norm_gain,
        norm_bias,
        layer_scale,
        out_bias,
    )
    vec = g_vec.reshape(4, 2, 2, 128)
    return (
        out_tokens,
        grad_tokens,
        jnp.swapaxes(g_qkv.reshape(2, 3 * HD, 128), 1, 2)[:, :, None, :],
        g_shift[:, None, :],
        g_out[:, None],
        g_fc1,
        g_unit,
        g_fc2,
        vec[0],
        vec[1],
        vec[2],
        vec[3],
    )


def solution(mesh):
    split = Mesh(
        mesh.devices.reshape(mesh.shape["fsdp"], NX, NZ, 2),
        ("fsdp", "tensor_0", "tensor_1", "tensor_2"),
    )
    return jax.shard_map(
        on_device,
        mesh=split,
        in_specs=(
            P(FSDP_TENSOR, None),
            P(FSDP_TENSOR, None),
            P(None, "fsdp", TENSOR, None),
            P(None, TENSOR, None),
            P(None, TENSOR, None, "fsdp"),
            P(None, "fsdp", TENSOR),
            P(None, TENSOR),
            P(None, TENSOR, "fsdp"),
            P(None, None, "fsdp"),
            P(None, None, "fsdp"),
            P(None, None, "fsdp"),
            P(None, None, "fsdp"),
        ),
        out_specs=(
            P(FSDP_TENSOR, None),
            P(FSDP_TENSOR, None),
            P(None, "fsdp", TENSOR, None),
            P(None, TENSOR, None),
            P(None, TENSOR, None, "fsdp"),
            P(None, "fsdp", TENSOR),
            P(None, TENSOR),
            P(None, TENSOR, "fsdp"),
            P(None, None, "fsdp"),
            P(None, None, "fsdp"),
            P(None, None, "fsdp"),
            P(None, None, "fsdp"),
        ),
        check_vma=False,
    )
```
